256 devices in a mesh: sn: 64 (over z, x, core), br: 4 (over y).
Axes of the slice: x: 4, y: 4, z: 8, core: 2. Of those that a mesh axis runs over, the one named last changes fastest.
Arguments:
- anc_inverse: bfloat16 [64, 16, 16, 128, 128], P('sn')
- parent_panel: bfloat16 [64, 2048, 128], P('sn'), may hold values from -0.125 to 0.125
- parent_dinv: bfloat16 [64, 128, 128], P('sn')
- child_route: int32 [1536, 1], P('sn'), may hold values from 0 to 63; in each aligned block of 24 rows (0 to 23, 24 to 47, ...) at most 2 rows name the same one
- child_pattern: int32 [1536, 4], P('sn'), may hold values from 0 to 16, as said below
- child_panel: bfloat16 [1536, 512, 128], P('sn', 'br'), may hold values from -0.625 to 0.625
- child_dinv: bfloat16 [1536, 128, 128], P('sn', 'br')
Outputs:
- parent_below: bfloat16 [64, 2048, 128], P('sn', 'br')
- parent_diag: bfloat16 [64, 128, 128], P('sn', 'br')
- child_column: bfloat16 [1536, 512, 128], P('sn', 'br')
- child_diag: bfloat16 [1536, 128, 128], P('sn', 'br')
The draws below stay inside these ranges and needn't reach their ends.
Inputs may be any that keep to these rules, and one draw needn't show every extreme that they name: `child_route`: among the 24 children on one index of sn no parent is named more than 2 times, and on some indices one parent is named exactly 2 times. `child_pattern`: each row starts with 0 (the parent's own block row); its other entries are distinct and rising.
All inputs are finite; a program needn't handle non-finite values.
Results may differ from the reference program's by a relative error of at most 0.0043.
Values may be sent and summed in bfloat16 or wider, within the bound.
A program may use at most 192 MiB of HBM per device.

```python
import math
import jax
import jax.numpy as jnp
import numpy as np
from jax import lax

B = 128
R1 = 16
E = 17
R2 = 4
CH_DEV = 24
PARENTS = 64
CHILDREN = 1536
CAP = 2


def draw_anc_inverse(key, part):
    shape = (PARENTS, R1, R1, B, B)
    raw_draw = jax.random.normal(key, shape, jnp.float32)
    symmetric = (raw_draw + jnp.transpose(raw_draw, (0, 2, 1, 4, 3))) * (0.70710678 / jnp.sqrt(jnp.float32(E * B)))
    identity = jnp.eye(R1, dtype=jnp.float32)[:, :, None, None] * jnp.eye(B, dtype=jnp.float32)[None, None]
    return (symmetric + identity[None]).astype(jnp.bfloat16)


def symmetric_dinv(key, count):
    shape = (count, B, B)
    raw_draw = jax.random.normal(key, shape, jnp.float32)
    symmetric = (raw_draw + jnp.swapaxes(raw_draw, 1, 2)) * 0.0212132
    return (symmetric + jnp.eye(B, dtype=jnp.float32)[None]).astype(jnp.bfloat16)


def draw_parent_dinv(key, part):
    return symmetric_dinv(key, PARENTS)


def draw_child_dinv(key, part):
    return symmetric_dinv(key, CHILDREN)


def pick_rows(subkey):
    return jax.random.permutation(subkey, E - 1)[:R2 - 1]


def draw_child_pattern(key, part):
    subkeys = jax.random.split(key, CHILDREN)
    chosen = jnp.sort(jax.vmap(pick_rows)(subkeys).astype(jnp.int32) + 1, axis=1)
    highest = jnp.arange(E - R2 + 1, E, dtype=jnp.int32)
    first_rows = (jnp.arange(CHILDREN) % CH_DEV == 0)[:, None]
    chosen = jnp.where(first_rows, highest[None, :], chosen)
    return jnp.concatenate([jnp.zeros((CHILDREN, 1), jnp.int32), chosen], axis=1)


def block_levels(key, shape, cuts, low, high):
    factor_of = 1.0
    for position, blocks in cuts:
        steps = jax.random.uniform(jax.random.fold_in(jax.random.fold_in(key, 6), position), (blocks,), jnp.float32, low / len(cuts), high / len(cuts))
        factor_of = factor_of * jnp.repeat(jnp.exp(steps), shape[position] // blocks).reshape((-1,) + (1,) * (len(shape) - 1 - position))
    return factor_of


def shared_out(rng, own, number, rows, number_of, top, bound, slope):
    ranking = jax.random.permutation(rng, number_of)
    packed, ordinary = load_shares(number_of, rows * top, bound, slope, True), load_shares(number_of, rows * top, bound, slope, False)
    places = jnp.arange(number_of)

    def named(lengths, turn):
        used = int((lengths > 0).sum())
        fixed = max(1, used // 4)
        shifted = fixed + (places - fixed + turn * (used - fixed)) % max(1, number_of - fixed)
        return jnp.zeros((number_of,), jnp.int32).at[ranking[jnp.where(places < fixed, places, shifted)]].set(jnp.asarray(lengths, jnp.int32))

    lengths = jnp.where(number % 4 == 0, named(packed, number // 4), named(ordinary, number - number // 4 - 1))
    mixed = jax.random.permutation(jax.random.fold_in(own, 3), number_of)
    donor, taker = mixed[0:number_of // 2 * 2:2], mixed[1:number_of // 2 * 2:2]
    slack = jnp.minimum(lengths[donor] - 1, bound - lengths[taker]) // 2
    slack = jnp.where((donor == ranking[0]) | (taker == ranking[0]) | (lengths[taker] == 0), 0, jnp.maximum(slack, 0))
    shifted = jax.random.randint(jax.random.fold_in(own, 4), (number_of // 2,), 0, 1 << 20) % (slack + 1)
    lengths = lengths.at[donor].add(-shifted).at[taker].add(shifted)
    labels = jnp.searchsorted(jnp.cumsum(lengths), jnp.arange(rows * top), side="right").astype(jnp.int32)
    grid = labels.reshape(top, rows).T
    grid = grid[jax.random.permutation(jax.random.fold_in(own, 1), rows)]
    turn = jax.random.randint(jax.random.fold_in(own, 2), (rows, 1), 0, top)
    return jnp.take_along_axis(grid, (jnp.arange(top)[None, :] + turn) % top, axis=1)


def load_shares(number_of, total, most, skew, full):
    loads = [(1 << 20) // math.isqrt(rank ** skew) + 1 for rank in range(1, number_of + 1)]
    largest = most if full else min(most, max(-(-total // number_of), total * loads[0] // sum(loads)))
    least = 1 if total - largest >= number_of - 1 else 0
    counts, rest = [largest] + [least] * (number_of - 1), total - largest - least * (number_of - 1)
    while rest > 0:
        free = [i for i in range(1, number_of) if counts[i] < largest] or [i for i in range(1, number_of) if counts[i] < most]
        whole, left = sum([loads[i] for i in free]), rest
        for i in free:
            more = min(most - counts[i], max(1, left * loads[i] // whole), rest)
            counts[i] = counts[i] + more
            rest = rest - more
    return np.array(counts)


def noise(own_key, dims, scale, limit, pieces=(), held_as=jnp.bfloat16):
    result = scale * jax.random.normal(own_key, dims, jnp.float32)
    if pieces:
        result = result * block_levels(own_key, dims, pieces, -0.22, 0.18)
    return jnp.clip(result, -limit, limit).astype(held_as)


def setup_inputs(seed: int = 0) -> dict:
    key_list = jax.random.split(jax.random.key(seed), 8)
    anc_inverse = draw_anc_inverse(jax.random.fold_in(key_list[7], 71), 0)
    parent_panel = noise(key_list[1], (PARENTS, R1 * B, B), (R1 * B) ** -0.5, 0.125, ((0, 64),))
    parent_dinv = draw_parent_dinv(jax.random.fold_in(key_list[7], 71), 0)
    child_route_keys = jax.random.split(jax.random.fold_in(key_list[3], 1), CHILDREN // CH_DEV)
    child_route_turns = jax.random.permutation(jax.random.fold_in(key_list[3], 3), CHILDREN // CH_DEV)
    child_route = jax.vmap(lambda own, number: shared_out(jax.random.fold_in(key_list[3], 2), own, number, CH_DEV, PARENTS, 1, CAP, 2))(child_route_keys, child_route_turns).reshape((CHILDREN, 1))
    child_pattern = draw_child_pattern(jax.random.fold_in(key_list[7], 71), 0)
    child_panel = noise(key_list[5], (CHILDREN, R2 * B, B), 0.1, 0.625, ((0, 64), (1, 4)))
    child_dinv = draw_child_dinv(jax.random.fold_in(key_list[7], 71), 0)
    return {"anc_inverse": anc_inverse, "parent_panel": parent_panel, "parent_dinv": parent_dinv, "child_route": child_route, "child_pattern": child_pattern, "child_panel": child_panel, "child_dinv": child_dinv}


def parent_step(items):
    anc_blocks, panel_flat, dinv_block = items
    panel_blocks = panel_flat.reshape(R1, B, B).astype(jnp.float32)
    below_col = (-jnp.einsum('kqab,qbc->kac', anc_blocks.astype(jnp.float32), panel_blocks)).astype(jnp.bfloat16)
    diag_block = (dinv_block.astype(jnp.float32) - jnp.einsum('kba,kbc->ac', panel_blocks, below_col.astype(jnp.float32))).astype(jnp.bfloat16)
    first_row = jnp.concatenate([diag_block[None], jnp.swapaxes(below_col, 1, 2)], axis=0)
    lower_rows = jnp.concatenate([below_col[:, None], anc_blocks], axis=1)
    full_inverse = jnp.concatenate([first_row[None], lower_rows], axis=0)
    return below_col.reshape(R1 * B, B), diag_block, full_inverse


def reference(anc_inverse, parent_panel, parent_dinv, child_route, child_pattern, child_panel, child_dinv):
    parent_below, parent_diag, full_all = lax.map(parent_step, (anc_inverse, parent_panel, parent_dinv))

    def child_step(items):
        route_rows, pattern_rows, panel_flat, dinv_rows = items
        panel_blocks = panel_flat.reshape(CH_DEV, R2, B, B).astype(jnp.float32)
        picked = full_all[route_rows[:, 0][:, None, None], pattern_rows[:, :, None], pattern_rows[:, None, :]]
        column = (-jnp.einsum('ckqab,cqbd->ckad', picked.astype(jnp.float32), panel_blocks)).astype(jnp.bfloat16)
        diag_rows = (dinv_rows.astype(jnp.float32) - jnp.einsum('ckba,ckbd->cad', panel_blocks, column.astype(jnp.float32))).astype(jnp.bfloat16)
        return column.reshape(CH_DEV, R2 * B, B), diag_rows

    groups = CHILDREN // CH_DEV
    columns, diags = lax.map(child_step, (child_route.reshape(groups, CH_DEV, 1), child_pattern.reshape(groups, CH_DEV, R2), child_panel.reshape(groups, CH_DEV, R2 * B, B), child_dinv.reshape(groups, CH_DEV, B, B)))
    return parent_below, parent_diag, columns.reshape(CHILDREN, R2 * B, B), diags.reshape(CHILDREN, B, B)
```

```python
import functools

import jax
import jax.numpy as jnp
from jax import lax
from jax.experimental import pallas as pl
from jax.experimental.pallas import tpu as pltpu
from jax.sharding import PartitionSpec as P

NZ = 8
NXC = 8
NB = 4
CAP = 2
MESH = pl.DeviceIdType.MESH
BF16 = jnp.bfloat16
F32 = jnp.float32


def place():
    sn = lax.axis_index("sn")
    return lax.div(sn, NXC), lax.rem(sn, NXC), lax.axis_index("br")


def greet():
    z, xc, k = place()
    barrier = pltpu.get_barrier_semaphore()

    def along_z(d, carry):
        pl.semaphore_signal(
            barrier, inc=1, device_id=(lax.rem(z + d, NZ) * NXC + xc, k), device_id_type=MESH
        )
        return carry

    def in_plane(o, carry):
        other = lax.rem(xc + lax.div(o, NB), NXC)
        pl.semaphore_signal(
            barrier,
            inc=1,
            device_id=(z * NXC + other, lax.rem(k + lax.rem(o, NB), NB)),
            device_id_type=MESH,
        )
        return carry

    lax.fori_loop(1, NZ, along_z, 0)
    lax.fori_loop(1, NXC * NB, in_plane, 0)
    pl.semaphore_wait(barrier, NZ - 1 + NXC * NB - 1)


def send_kernel(
    slots, z_child, x_pick, panel, x_out, z_send, x_send, z_got, zs_sem, zr_sem, xs_sem, xr_sem
):
    z, xc, k = place()
    greet()

    def z_copy(dz):
        return pltpu.make_async_remote_copy(
            src_ref=z_send.at[dz],
            dst_ref=z_got[dz],
            send_sem=zs_sem.at[dz],
            recv_sem=zr_sem.at[dz],
            device_id=(lax.rem(z + dz, NZ) * NXC + xc, k),
            device_id_type=MESH,
        )

    for dz in (1, 7, 2, 6, 3, 5, 4):

        def fill(j, carry, dz=dz):
            z_send[dz, j] = panel[z_child[dz, j]]
            return carry

        lax.fori_loop(0, slots, fill, 0)
        z_copy(dz).start()

    def own(j, carry):
        z_got[0][j] = panel[z_child[0, j]]
        return carry

    lax.fori_loop(0, slots, own, 0)

    for dz in (0, 1, 7, 2, 6, 3, 5, 4):
        if dz:
            z_copy(dz).wait_recv()
        half, target = dz // NB, dz % NB

        def forward(o, carry, dz=dz, half=half, target=target):
            other = lax.rem(xc + o, NXC)
            for rank in range(CAP):
                x_send[dz * NXC + other, rank] = z_got[dz][x_pick[dz, other * CAP + rank]]
            here = jnp.logical_and(o == 0, k == target)

            @pl.when(here)
            def _():
                pltpu.make_async_copy(
                    x_send.at[dz * NXC + other], x_out.at[half, xc, k], xr_sem
                ).start()

            @pl.when(jnp.logical_not(here))
            def _():
                pltpu.make_async_remote_copy(
                    src_ref=x_send.at[dz * NXC + other],
                    dst_ref=x_out.at[half, xc, k],
                    send_sem=xs_sem,
                    recv_sem=xr_sem,
                    device_id=(z * NXC + other, target),
                    device_id_type=MESH,
                ).start()

            return carry

        lax.fori_loop(0, NXC, forward, 0)

    for dz in range(1, NZ):
        z_copy(dz).wait_send()
    remote = pl.ds(0, NZ * NXC - NZ // NB)
    pltpu.make_async_copy(x_send.at[remote], x_send.at[remote], xs_sem).wait()
    pltpu.make_async_copy(x_out, x_out, xr_sem).wait()


def send_children(slots, ident, z_child, x_pick, panel_blocks):
    width = panel_blocks.shape[-1]
    block = (width, width)
    smem = pl.BlockSpec(memory_space=pltpu.SMEM)
    return pl.pallas_call(
        functools.partial(send_kernel, slots),
        out_shape=jax.ShapeDtypeStruct((NZ // NB, NXC, NB, CAP) + block, BF16),
        in_specs=[smem, smem, pl.BlockSpec(memory_space=pltpu.VMEM)],
        out_specs=pl.BlockSpec(memory_space=pl.ANY),
        scratch_shapes=[
            pltpu.VMEM((NZ, slots) + block, BF16),
            pltpu.VMEM((NZ * NXC, CAP) + block, BF16),
            [pltpu.VMEM((slots,) + block, BF16) for _ in range(NZ)],
            pltpu.SemaphoreType.DMA((NZ,)),
            pltpu.SemaphoreType.DMA((NZ,)),
            pltpu.SemaphoreType.DMA,
            pltpu.SemaphoreType.DMA,
        ],
        compiler_params=pltpu.CompilerParams(
            collective_id=ident, has_side_effects=True, vmem_limit_bytes=40 * 2**20
        ),
    )(z_child, x_pick, panel_blocks)


def return_kernel(
    slots, z_pick, child_slot, y, column, z_back, z_home, y_got, ys_sem, yr_sem, zs_sem, zr_sem
):
    z, xc, k = place()
    greet()

    for dz in (4, 3, 5, 2, 6, 1, 7, 0):
        half = dz // NB

        @pl.when(k == dz % NB)
        def _(dz=dz, half=half):
            def scatter(o, carry):
                other = lax.rem(xc + lax.div(o, NB), NXC)
                row = lax.rem(k + lax.rem(o, NB), NB)

                @pl.when(o == 0)
                def _():
                    pltpu.make_async_copy(
                        y.at[half, other, row], y_got[dz].at[pl.ds(xc * CAP, CAP)], yr_sem.at[dz]
                    ).start()

                @pl.when(o > 0)
                def _():
                    pltpu.make_async_remote_copy(
                        src_ref=y.at[half, other, row],
                        dst_ref=y_got[dz].at[pl.ds(xc * CAP, CAP)],
                        send_sem=ys_sem,
                        recv_sem=yr_sem.at[dz],
                        device_id=(z * NXC + other, row),
                        device_id_type=MESH,
                    ).start()

                return carry

            lax.fori_loop(0, NXC * NB, scatter, 0)

    def z_copy(dz):
        return pltpu.make_async_remote_copy(
            src_ref=z_back.at[dz],
            dst_ref=z_home.at[pl.ds(dz * slots, slots)],
            send_sem=zs_sem.at[dz],
            recv_sem=zr_sem.at[dz],
            device_id=(lax.rem(z + NZ - dz, NZ) * NXC + xc, k),
            device_id_type=MESH,
        )

    for dz in (4, 3, 5, 2, 6, 1, 7, 0):
        pltpu.make_async_copy(y_got[dz], y_got[dz], yr_sem.at[dz]).wait()

        def pack(j, carry, dz=dz):
            if dz:
                z_back[dz, j] = y_got[dz][z_pick[dz, j]]
            else:
                z_home[j] = y_got[dz][z_pick[dz, j]]
            return carry

        lax.fori_loop(0, slots, pack, 0)
        if dz:
            z_copy(dz).start()

    for dz in range(1, NZ):
        z_copy(dz).wait_recv()

    def unpack(i, carry):
        column[i] = z_home[child_slot[i]]
        return carry

    lax.fori_loop(0, column.shape[0], unpack, 0)
    for dz in range(1, NZ):
        z_copy(dz).wait_send()
    sent = NXC * NB - 1
    for half in range(NZ // NB):
        flat = y.at[half, pl.ds(0, NXC - 1)]
        pltpu.make_async_copy(flat, flat, ys_sem).wait()
        last = y.at[half, NXC - 1, pl.ds(0, sent - (NXC - 1) * NB)]
        pltpu.make_async_copy(last, last, ys_sem).wait()


def return_children(slots, ident, z_pick, child_slot, y):
    block = y.shape[-2:]
    smem = pl.BlockSpec(memory_space=pltpu.SMEM)
    count = child_slot.shape[0]
    return pl.pallas_call(
        functools.partial(return_kernel, slots),
        out_shape=jax.ShapeDtypeStruct((count,) + block, BF16),
        in_specs=[smem, smem, pl.BlockSpec(memory_space=pl.ANY)],
        out_specs=pl.BlockSpec(memory_space=pltpu.VMEM),
        scratch_shapes=[
            pltpu.VMEM((NZ, slots) + block, BF16),
            pltpu.VMEM((NZ * slots,) + block, BF16),
            [pltpu.VMEM((NXC * CAP,) + block, BF16) for _ in range(NZ)],
            pltpu.SemaphoreType.DMA,
            pltpu.SemaphoreType.DMA((NZ,)),
            pltpu.SemaphoreType.DMA((NZ,)),
            pltpu.SemaphoreType.DMA((NZ,)),
        ],
        compiler_params=pltpu.CompilerParams(
            collective_id=ident, has_side_effects=True, vmem_limit_bytes=40 * 2**20
        ),
    )(z_pick, child_slot, y)


def parent_kernel(
    pattern, anc, parent_blocks, dinv, x, below_out, diag_out, y, full, sem
):
    ancestors, width = parent_blocks.shape[0], parent_blocks.shape[-1]
    row = lax.axis_index("br")
    for k in range(ancestors):
        pltpu.make_async_copy(
            anc.at[k], full.at[k + 1, pl.ds(1, ancestors)], sem.at[k]
        ).start()
    diag = dinv[...].astype(F32)
    for k in range(ancestors):
        pltpu.make_async_copy(
            anc.at[k], full.at[k + 1, pl.ds(1, ancestors)], sem.at[k]
        ).wait()
        total = jnp.zeros((width, width), F32)
        for l in range(0, ancestors, 4):
            left = jnp.concatenate([full[k + 1, 1 + l + i] for i in range(4)], axis=1)
            right = jnp.concatenate([parent_blocks[l + i] for i in range(4)], axis=0)
            total += jnp.dot(left, right, preferred_element_type=F32)
        total = (-total).astype(BF16)
        full[k + 1, 0] = total
        full[0, k + 1] = total.T
        diag -= lax.dot_general(
            parent_blocks[k], total, (((0,), (0,)), ((), ())), preferred_element_type=F32
        )
    full[0, 0] = diag.astype(BF16)
    share = ancestors // NB
    for i in range(share):
        below_out[i] = full[1 + row * share + i, 0]
    diag_out[...] = full[0, 0, pl.ds(row * (width // NB), width // NB)]

    def child(n, carry):
        group, rank = lax.div(n, CAP), lax.rem(n, CAP)
        half, xc = lax.div(group, NXC), lax.rem(group, NXC)
        spot = [pattern[n, k] for k in range(NB)]
        right = jnp.concatenate([x[half, xc, l, rank] for l in range(NB)], axis=0)
        for k in range(NB):
            left = jnp.concatenate([full[spot[k], spot[l]] for l in range(NB)], axis=1)
            y[half, xc, k, rank] = (-jnp.dot(left, right, preferred_element_type=F32)).astype(BF16)
        return carry

    lax.fori_loop(0, NZ // NB * NXC * CAP, child, 0)


def parent_step(pattern, anc, parent_blocks, dinv, x):
    ancestors, width = parent_blocks.shape[0], parent_blocks.shape[-1]
    vmem = pl.BlockSpec(memory_space=pltpu.VMEM)
    return pl.pallas_call(
        parent_kernel,
        out_shape=(
            jax.ShapeDtypeStruct((ancestors // NB, width, width), BF16),
            jax.ShapeDtypeStruct((width // NB, width), BF16),
            jax.ShapeDtypeStruct(x.shape, BF16),
        ),
        in_specs=[
            pl.BlockSpec(memory_space=pltpu.SMEM),
            pl.BlockSpec(memory_space=pl.ANY),
            vmem,
            vmem,
            vmem,
        ],
        out_specs=(vmem, vmem, vmem),
        scratch_shapes=[
            pltpu.VMEM((ancestors + 1, ancestors + 1, width, width), BF16),
            pltpu.SemaphoreType.DMA((ancestors,)),
        ],
        compiler_params=pltpu.CompilerParams(vmem_limit_bytes=40 * 2**20),
    )(pattern, anc, parent_blocks, dinv, x)


def tables(child_route, child_pattern):
    z, xc, row = place()
    count = child_route.shape[0]
    meta = jnp.concatenate([child_route, child_pattern], axis=1).reshape(-1)
    meta = lax.all_gather(meta, "sn").reshape(NZ, NXC, count, -1)
    route, pattern = meta[..., 0], meta[..., 1:]
    goal = route // NXC
    earlier = jnp.tri(count, k=-1, dtype=jnp.bool_)
    spot = jnp.sum(((goal[..., :, None] == goal[..., None, :]) & earlier).astype(jnp.int32), -1)
    rank = jnp.sum(((route[..., :, None] == route[..., None, :]) & earlier).astype(jnp.int32), -1)
    fullest = jnp.max(spot) + 1
    most = NXC * CAP

    def own(values):
        return lax.dynamic_slice(values, (z, xc, 0), (1, 1, count))[0, 0]

    step = lax.rem(own(goal) - z + NZ, NZ)
    own_spot = own(spot)
    steps = jnp.arange(NZ, dtype=jnp.int32)
    places = jnp.arange(most, dtype=jnp.int32)
    hit = (step == steps[:, None, None]) & (own_spot == places[:, None])
    z_child = jnp.sum(jnp.where(hit, jnp.arange(count, dtype=jnp.int32), 0), -1)

    sources = lax.rem(z - steps + NZ, NZ)

    def column_of(values):
        return lax.dynamic_index_in_dim(values, xc, 1, keepdims=False)[sources]

    mine = column_of(goal) == z
    target = (column_of(route) % NXC) * CAP + column_of(rank)
    via = column_of(spot)
    hit = (mine & True)[:, None] & (target[:, None] == places[:, None])
    x_pick = jnp.sum(jnp.where(hit, via[:, None], 0), -1)
    hit = mine[:, None] & (via[:, None] == places[:, None])
    z_pick = jnp.sum(jnp.where(hit, target[:, None], 0), -1)

    parts = sources.reshape(NZ // NB, NB)[:, row]
    here = (route == z * NXC + xc)[parts]
    hit = here[:, :, None] & (rank[parts][:, :, None] == jnp.arange(CAP)[:, None])
    child_spots = jnp.sum(jnp.where(hit[..., None], pattern[parts][:, :, None], 0), -2)
    return fullest, z_child, x_pick, z_pick, step, own_spot, child_spots.reshape(-1, NB)


def on_device(
    anc_inverse, parent_panel, parent_dinv, child_route, child_pattern, child_panel, child_dinv
):
    width = parent_dinv.shape[-1]
    ancestors = anc_inverse.shape[1]
    count = child_route.shape[0]
    few, most = NXC, NXC * CAP
    panel_blocks = child_panel.reshape(count, width, width)
    parent_blocks = parent_panel[0].reshape(ancestors, width, width)
    fullest, z_child, x_pick, z_pick, step, own_spot, child_spots = tables(
        child_route, child_pattern
    )
    fits = fullest <= few
    x = lax.cond(
        fits,
        functools.partial(send_children, few, 1),
        functools.partial(send_children, most, 2),
        z_child,
        x_pick,
        panel_blocks,
    )
    below, diag, y = parent_step(child_spots, anc_inverse[0], parent_blocks, parent_dinv[0], x)
    column = lax.cond(
        fits,
        lambda a, b, c, d: return_children(few, 3, a, b * few + c, d),
        lambda a, b, c, d: return_children(most, 4, a, b * most + c, d),
        z_pick,
        step,
        own_spot,
        y,
    )
    term = jnp.einsum("cba,cbd->cad", panel_blocks, column, preferred_element_type=F32)
    summed = lax.psum_scatter(term, "br", scatter_dimension=1, tiled=True)
    child_diag = (child_dinv.astype(F32) - summed).astype(BF16)
    return (below.reshape(1, -1, width), diag[None], column, child_diag)


def solution(mesh):
    placed = (
        P("sn", None, None, None, None),
        P("sn", None, None),
        P("sn", None, None),
        P("sn", None),
        P("sn", None),
        P("sn", "br", None),
        P("sn", "br", None),
    )
    return jax.shard_map(
        on_device,
        mesh=mesh,
        in_specs=placed,
        out_specs=(
            P("sn", "br", None),
            P("sn", "br", None),
            P("sn", "br", None),
            P("sn", "br", None),
        ),
        check_vma=False,
    )
```

```python
import functools

import jax
import jax.numpy as jnp
from jax import lax
from jax.experimental import pallas as pl
from jax.experimental.pallas import tpu as pltpu
from jax.sharding import PartitionSpec as P

NZ = 8
NXC = 8
NB = 4
CAP = 2
MESH = pl.DeviceIdType.MESH
BF16 = jnp.bfloat16
F32 = jnp.float32


STEPS = (0, 1, 7, 2, 6, 3, 5, 4)
HALVES = NZ // NB
PICKS = NXC * CAP
Z_CHILD = 0
X_PICK = Z_CHILD + NZ * PICKS
Z_PICK = X_PICK + NZ * PICKS
SPOTS = Z_PICK + NZ * PICKS
SLOT = SPOTS + NZ * PICKS * NB


def place():
    sn = lax.axis_index("sn")
    return lax.div(sn, NXC), lax.rem(sn, NXC), lax.axis_index("br")


def signal(sn, row):
    pl.semaphore_signal(
        pltpu.get_barrier_semaphore(), inc=1, device_id=(sn, row), device_id_type=MESH
    )


def routes_kernel(meta, out, send_sem, near_sem, far_sem):
    z, xc, k = place()

    def mate_z(d):
        return lax.rem(z + d, NZ) * NXC + xc

    def mate_xc(d):
        return z * NXC + lax.rem(xc + d, NXC)

    for d in range(1, NZ):
        signal(mate_z(d), k)
    for d in range(1, NXC):
        signal(mate_xc(d), k)
    pl.semaphore_wait(pltpu.get_barrier_semaphore(), NZ + NXC - 2)

    pltpu.make_async_copy(meta, out.at[xc, z], near_sem).start()
    for d in range(1, NZ):
        pltpu.make_async_remote_copy(
            src_ref=meta,
            dst_ref=out.at[xc, z],
            send_sem=send_sem.at[0],
            recv_sem=near_sem,
            device_id=(mate_z(d), k),
            device_id_type=MESH,
        ).start()
    pltpu.make_async_copy(out.at[xc], out.at[xc], near_sem).wait()
    for d in range(1, NXC):
        pltpu.make_async_remote_copy(
            src_ref=out.at[xc],
            dst_ref=out.at[xc],
            send_sem=send_sem.at[1],
            recv_sem=far_sem,
            device_id=(mate_xc(d), k),
            device_id_type=MESH,
        ).start()
    some = out.at[pl.ds(0, NXC - 1)]
    pltpu.make_async_copy(some, some, far_sem).wait()
    part = out.at[0, pl.ds(0, NZ - 1)]
    pltpu.make_async_copy(part, part, send_sem.at[0]).wait()
    pltpu.make_async_copy(some, some, send_sem.at[1]).wait()


def all_routes(meta):
    vmem = pl.BlockSpec(memory_space=pltpu.VMEM)
    return pl.pallas_call(
        routes_kernel,
        out_shape=jax.ShapeDtypeStruct((NXC, NZ) + meta.shape, meta.dtype),
        in_specs=[vmem],
        out_specs=vmem,
        scratch_shapes=[
            pltpu.SemaphoreType.DMA((2,)),
            pltpu.SemaphoreType.DMA,
            pltpu.SemaphoreType.DMA,
        ],
        compiler_params=pltpu.CompilerParams(collective_id=1, has_side_effects=True),
    )(meta)


def greet():
    z, xc, k = place()

    def along_z(d, carry):
        signal(lax.rem(z + d, NZ) * NXC + xc, k)
        return carry

    def in_plane(o, carry):
        signal(
            z * NXC + lax.rem(xc + lax.div(o, NB), NXC), lax.rem(k + lax.rem(o, NB), NB)
        )
        return carry

    lax.fori_loop(1, NZ, along_z, 0)
    lax.fori_loop(1, NXC * NB, in_plane, 0)
    pl.semaphore_wait(pltpu.get_barrier_semaphore(), NZ - 1 + NXC * NB - 1)


def whole_kernel(
    slots,
    table,
    panel,
    anc,
    parent_blocks,
    dinv,
    child_dinv,
    below_out,
    diag_out,
    column,
    child_diag,
    full,
    z_send,
    x_send,
    x,
    y,
    z_home,
    t_send,
    t_got,
    z_got,
    y_got,
    f_sem,
    zs_sem,
    zr_sem,
    xs_sem,
    xr_sem,
    ys_sem,
    yr_sem,
    hs_sem,
    hr_sem,
    ts_sem,
    tr_sem,
):
    z, xc, k = place()
    ancestors, width = parent_blocks.shape[0], parent_blocks.shape[-1]
    rows = width // NB
    count = column.shape[0]
    share = ancestors // NB
    plane = lax.rem(k - xc + 2 * NB, NB)

    def full_copy(i):
        return pltpu.make_async_copy(
            anc.at[i], full.at[i + 1, pl.ds(1, ancestors)], f_sem.at[i]
        )

    for i in range(ancestors):
        full_copy(i).start()
    greet()

    def ahead(n):
        return lax.rem(z + STEPS[n], NZ)

    def behind(n):
        return lax.rem(z + NZ - STEPS[n], NZ)

    def z_copy(n):
        return pltpu.make_async_remote_copy(
            src_ref=z_send.at[n],
            dst_ref=z_got[n],
            send_sem=zs_sem.at[n],
            recv_sem=zr_sem.at[n],
            device_id=(ahead(n) * NXC + xc, k),
            device_id_type=MESH,
        )

    for n in range(1, NZ):

        def fill(j, carry, n=n):
            z_send[n, j] = panel[table[Z_CHILD + ahead(n) * PICKS + j]]
            return carry

        lax.fori_loop(0, slots, fill, 0)
        z_copy(n).start()

    def own(j, carry):
        z_got[0][j] = panel[table[Z_CHILD + z * PICKS + j]]
        return carry

    lax.fori_loop(0, slots, own, 0)

    def forward(n):
        if n:
            z_copy(n).wait_recv()

        def step(o, carry):
            other = lax.rem(xc + o, NXC)
            target = lax.rem(other + n, NB)
            for rank in range(CAP):
                pick = table[X_PICK + behind(n) * PICKS + other * CAP + rank]
                x_send[n * NXC + other, rank] = z_got[n][pick]
            here = jnp.logical_and(o == 0, k == target)

            @pl.when(here)
            def _():
                pltpu.make_async_copy(
                    x_send.at[n * NXC + other], x.at[n // NB, xc, k], xr_sem.at[n // NB]
                ).start()

            @pl.when(jnp.logical_not(here))
            def _():
                pltpu.make_async_remote_copy(
                    src_ref=x_send.at[n * NXC + other],
                    dst_ref=x.at[n // NB, xc, k],
                    send_sem=xs_sem,
                    recv_sem=xr_sem.at[n // NB],
                    device_id=(z * NXC + other, target),
                    device_id_type=MESH,
                ).start()

            return carry

        lax.fori_loop(0, NXC, step, 0)

    def parent():
        diag = dinv[...].astype(F32)
        for i in range(ancestors):
            full_copy(i).wait()
            total = jnp.zeros((width, width), F32)
            for l in range(0, ancestors, NB):
                left = jnp.concatenate([full[i + 1, 1 + l + m] for m in range(NB)], axis=1)
                right = jnp.concatenate([parent_blocks[l + m] for m in range(NB)], axis=0)
                total += jnp.dot(left, right, preferred_element_type=F32)
            total = (-total).astype(BF16)
            full[i + 1, 0] = total
            full[0, i + 1] = total.T
            diag -= lax.dot_general(
                parent_blocks[i], total, (((0,), (0,)), ((), ())), preferred_element_type=F32
            )
        full[0, 0] = diag.astype(BF16)
        for i in range(share):
            below_out[i] = full[1 + k * share + i, 0]
        diag_out[...] = full[0, 0, pl.ds(k * rows, rows)]

    def children(half):
        step = jnp.int32(0)
        for p in range(NB):
            step = jnp.where(plane == p, STEPS[half * NB + p], step)
        source = lax.rem(z + NZ - step, NZ)
        pltpu.make_async_copy(x.at[half], x.at[half], xr_sem.at[half]).wait()

        def group(o, carry):
            other = lax.rem(xc + o, NXC)
            first = half * NXC * NB + other * NB
            for rank in range(CAP):
                base = SPOTS + ((source * NXC + other) * CAP + rank) * NB
                spot = [table[base + l] for l in range(NB)]
                right = jnp.concatenate([x[half, other, l, rank] for l in range(NB)], axis=0)
                for i in range(NB):
                    left = jnp.concatenate([full[spot[i], spot[l]] for l in range(NB)], axis=1)
                    product = jnp.dot(left, right, preferred_element_type=F32)
                    y[first + i, rank] = (-product).astype(BF16)
            for p in range(NB):
                landing = y_got[half * NB + p]
                arrived = yr_sem.at[half * NB + p]

                @pl.when(plane == p)
                def _(landing=landing, arrived=arrived):
                    def back(i, carry):
                        row = lax.rem(k + i, NB)
                        here = jnp.logical_and(o == 0, i == 0)

                        @pl.when(here)
                        def _():
                            pltpu.make_async_copy(
                                y.at[first + row], landing.at[pl.ds(xc * CAP, CAP)], arrived
                            ).start()

                        @pl.when(jnp.logical_not(here))
                        def _():
                            pltpu.make_async_remote_copy(
                                src_ref=y.at[first + row],
                                dst_ref=landing.at[pl.ds(xc * CAP, CAP)],
                                send_sem=ys_sem,
                                recv_sem=arrived,
                                device_id=(z * NXC + other, row),
                                device_id_type=MESH,
                            ).start()

                        return carry

                    lax.fori_loop(0, NB, back, 0)

            return carry

        lax.fori_loop(0, NXC, group, 0)

    def home_copy(n, zone):
        return pltpu.make_async_remote_copy(
            src_ref=z_send.at[n],
            dst_ref=z_home.at[pl.ds(zone * slots, slots)],
            send_sem=hs_sem.at[n],
            recv_sem=hr_sem.at[n],
            device_id=(behind(n) * NXC + xc, k),
            device_id_type=MESH,
        )

    def backward(n):
        pltpu.make_async_copy(y_got[n], y_got[n], yr_sem.at[n]).wait()
        if n:
            z_copy(n).wait_send()

        def pack(j, carry):
            block = y_got[n][table[Z_PICK + behind(n) * PICKS + j]]
            if n:
                z_send[n, j] = block
            else:
                z_home[z * slots + j] = block
            return carry

        lax.fori_loop(0, slots, pack, 0)
        if n:
            home_copy(n, z).start()

    parent()
    for n in range(NB):
        forward(n)
    children(0)
    for n in range(NB, NZ):
        forward(n)
    for n in range(NB):
        backward(n)
    children(1)
    for n in range(NB, NZ):
        backward(n)
    for n in range(1, NZ):
        home_copy(n, ahead(n)).wait_recv()

    batch = count // NB

    def term_copy(b, d):
        row = lax.rem(k + d, NB)
        return pltpu.make_async_remote_copy(
            src_ref=t_send.at[row, pl.ds(b * batch, batch)],
            dst_ref=t_got.at[k, pl.ds(b * batch, batch)],
            send_sem=ts_sem,
            recv_sem=tr_sem.at[b],
            device_id=(z * NXC + xc, row),
            device_id_type=MESH,
        )

    for b in range(NB):

        def unpack(i, carry):
            block = z_home[table[SLOT + i]]
            column[i] = block
            term = lax.dot_general(
                panel[i], block, (((0,), (0,)), ((), ())), preferred_element_type=F32
            )
            for q in range(NB):
                t_send[q, i] = term[q * rows : (q + 1) * rows]
            return carry

        lax.fori_loop(b * batch, (b + 1) * batch, unpack, 0)
        for d in range(1, NB):
            term_copy(b, d).start()

    for b in range(NB):
        got = t_got.at[pl.ds(0, NB - 1), pl.ds(b * batch, batch)]
        pltpu.make_async_copy(got, got, tr_sem.at[b]).wait()

        def finish(i, carry):
            total = t_send[k, i]
            for d in range(1, NB):
                total += t_got[lax.rem(k + d, NB), i]
            child_diag[i] = (child_dinv[i].astype(F32) - total).astype(BF16)
            return carry

        lax.fori_loop(b * batch, (b + 1) * batch, finish, 0)

    for n in range(1, NZ):
        home_copy(n, z).wait_send()
    remote = pl.ds(0, NZ * NXC - HALVES)
    pltpu.make_async_copy(x_send.at[remote], x_send.at[remote], xs_sem).wait()
    pltpu.make_async_copy(y.at[remote], y.at[remote], ys_sem).wait()
    sent = t_send.at[pl.ds(0, NB - 1)]
    pltpu.make_async_copy(sent, sent, ts_sem).wait()


def whole(slots, ident, table, panel_blocks, anc, parent_blocks, dinv, child_dinv):
    ancestors, width = parent_blocks.shape[0], parent_blocks.shape[-1]
    count, rows = panel_blocks.shape[0], width // NB
    block = (width, width)
    vmem = pl.BlockSpec(memory_space=pltpu.VMEM)
    dma = pltpu.SemaphoreType.DMA
    return pl.pallas_call(
        functools.partial(whole_kernel, slots),
        out_shape=(
            jax.ShapeDtypeStruct((ancestors // NB,) + block, BF16),
            jax.ShapeDtypeStruct((rows, width), BF16),
            jax.ShapeDtypeStruct((count,) + block, BF16),
            jax.ShapeDtypeStruct((count, rows, width), BF16),
        ),
        in_specs=[
            pl.BlockSpec(memory_space=pltpu.SMEM),
            vmem,
            pl.BlockSpec(memory_space=pl.ANY),
            vmem,
            vmem,
            vmem,
        ],
        out_specs=(vmem, vmem, vmem, vmem),
        scratch_shapes=[
            pltpu.VMEM((ancestors + 1, ancestors + 1) + block, BF16),
            pltpu.VMEM((NZ, slots) + block, BF16),
            pltpu.VMEM((NZ * NXC, CAP) + block, BF16),
            pltpu.VMEM((HALVES, NXC, NB, CAP) + block, BF16),
            pltpu.VMEM((HALVES * NXC * NB, CAP) + block, BF16),
            pltpu.VMEM((NZ * slots,) + block, BF16),
            pltpu.VMEM((NB, count, rows, width), F32),
            pltpu.VMEM((NB, count, rows, width), F32),
            [pltpu.VMEM((slots,) + block, BF16) for _ in range(NZ)],
            [pltpu.VMEM((PICKS,) + block, BF16) for _ in range(NZ)],
            dma((ancestors,)),
            dma((NZ,)),
            dma((NZ,)),
            dma,
            dma((HALVES,)),
            dma,
            dma((NZ,)),
            dma((NZ,)),
            dma((NZ,)),
            dma,
            dma((NB,)),
        ],
        compiler_params=pltpu.CompilerParams(
            collective_id=ident, has_side_effects=True, vmem_limit_bytes=56 * 2**20
        ),
    )(table, panel_blocks, anc, parent_blocks, dinv, child_dinv)


def tables(child_route, child_pattern):
    z, xc, _ = place()
    count = child_route.shape[0]
    meta = jnp.concatenate([child_route.reshape(-1), child_pattern.T.reshape(-1)])
    meta = jnp.pad(meta, (0, 8 * 128 - meta.shape[0])).reshape(8, 128)
    meta = all_routes(meta).reshape(NXC, NZ, -1)[..., : (1 + NB) * count]
    route = meta[..., :count]
    pattern = meta[..., count:].reshape(NXC, NZ, NB, count)
    goal = route // NXC
    earlier = jnp.arange(count)[None, :] < jnp.arange(count)[:, None]
    spot = jnp.sum(((goal[..., :, None] == goal[..., None, :]) & earlier).astype(jnp.int32), -1)
    rank = jnp.sum(((route[..., :, None] == route[..., None, :]) & earlier).astype(jnp.int32), -1)
    fullest = jnp.max(spot) + 1

    def of_xc(values):
        return lax.dynamic_index_in_dim(values, xc, 0, keepdims=False)

    places = jnp.arange(PICKS, dtype=jnp.int32)[:, None]
    route_xc, spot_xc, rank_xc = of_xc(route), of_xc(spot), of_xc(rank)
    goal_xc = route_xc // NXC
    own_goal = lax.dynamic_index_in_dim(goal_xc, z, 0, keepdims=False)
    own_spot = lax.dynamic_index_in_dim(spot_xc, z, 0, keepdims=False)
    hit = (own_goal == jnp.arange(NZ)[:, None, None]) & (own_spot == places)
    z_child = jnp.sum(jnp.where(hit, jnp.arange(count, dtype=jnp.int32), 0), -1)

    mine = (goal_xc == z)[:, None]
    target = ((route_xc % NXC) * CAP + rank_xc)[:, None]
    via = spot_xc[:, None]
    x_pick = jnp.sum(jnp.where(mine & (target == places), via, 0), -1)
    z_pick = jnp.sum(jnp.where(mine & (via == places), target, 0), -1)

    hit = (route == z * NXC + xc)[:, :, None] & (rank[:, :, None] == jnp.arange(CAP)[:, None])
    spots = jnp.sum(jnp.where(hit[:, :, :, None], pattern[:, :, None], 0), -1)
    spots = jnp.swapaxes(spots, 0, 1)

    def with_slots(slots):
        parts = (z_child, x_pick, z_pick, spots, own_goal * slots + own_spot)
        return jnp.concatenate([part.reshape(-1) for part in parts])

    return fullest, with_slots


def on_device(
    anc_inverse, parent_panel, parent_dinv, child_route, child_pattern, child_panel, child_dinv
):
    width = parent_dinv.shape[-1]
    ancestors = anc_inverse.shape[1]
    count = child_route.shape[0]
    few, most = NXC, PICKS
    fullest, with_slots = tables(child_route, child_pattern)
    fits = fullest <= few
    table = with_slots(jnp.where(fits, few, most))
    below, diag, column, child_diag = lax.cond(
        fits,
        functools.partial(whole, few, 2),
        functools.partial(whole, most, 3),
        table,
        child_panel.reshape(count, width, width),
        anc_inverse[0],
        parent_panel[0].reshape(ancestors, width, width),
        parent_dinv[0],
        child_dinv,
    )
    return (below.reshape(1, -1, width), diag[None], column, child_diag)


def solution(mesh):
    placed = (
        P("sn", None, None, None, None),
        P("sn", None, None),
        P("sn", None, None),
        P("sn", None),
        P("sn", None),
        P("sn", "br", None),
        P("sn", "br", None),
    )
    return jax.shard_map(
        on_device,
        mesh=mesh,
        in_specs=placed,
        out_specs=(
            P("sn", "br", None),
            P("sn", "br", None),
            P("sn", "br", None),
            P("sn", "br", None),
        ),
        check_vma=False,
    )
```

```python
import functools

import jax
import jax.numpy as jnp
from jax import lax
from jax.experimental import pallas as pl
from jax.experimental.pallas import tpu as pltpu
from jax.sharding import PartitionSpec as P

NZ = 8
NX = 4
CORES = 2
NXC = NX * CORES
NB = 4
CAP = 2
MESH = pl.DeviceIdType.MESH
BF16 = jnp.bfloat16
F32 = jnp.float32


STEPS = (0, 4, 2, 6, 1, 7, 3, 5)
AT_ONCE = 3
PICKS = NXC * CAP
PAIR = CORES * CAP
SIZES = ((6, 3), (7, 3), (8, 3), (PICKS, PAIR))
Z_CHILD = 0
X_PICK = Z_CHILD + NZ * PICKS
Z_PICK = X_PICK + NZ * PICKS
SPOTS = Z_PICK + NZ * PICKS
SPOT = 1 + NB
SLOT = SPOTS + NXC * PAIR * SPOT


def place():
    sn = lax.axis_index("sn")
    return lax.div(sn, NXC), lax.rem(sn, NXC), lax.axis_index("br")


def signal(sn, row):
    pl.semaphore_signal(
        pltpu.get_barrier_semaphore(), inc=1, device_id=(sn, row), device_id_type=MESH
    )


def routes_kernel(meta, out, send_sem, near_sem, far_sem):
    z, xc, k = place()

    def mate_z(d):
        return lax.rem(z + d, NZ) * NXC + xc

    def mate_xc(d):
        return z * NXC + lax.rem(xc + d, NXC)

    for d in range(1, NZ):
        signal(mate_z(d), k)
    for d in range(1, NXC):
        signal(mate_xc(d), k)
    pl.semaphore_wait(pltpu.get_barrier_semaphore(), NZ + NXC - 2)

    pltpu.make_async_copy(meta, out.at[xc, z], near_sem).start()
    for d in range(1, NZ):
        pltpu.make_async_remote_copy(
            src_ref=meta,
            dst_ref=out.at[xc, z],
            send_sem=send_sem.at[0],
            recv_sem=near_sem,
            device_id=(mate_z(d), k),
            device_id_type=MESH,
        ).start()
    pltpu.make_async_copy(out.at[xc], out.at[xc], near_sem).wait()
    for d in range(1, NXC):
        pltpu.make_async_remote_copy(
            src_ref=out.at[xc],
            dst_ref=out.at[xc],
            send_sem=send_sem.at[1],
            recv_sem=far_sem,
            device_id=(mate_xc(d), k),
            device_id_type=MESH,
        ).start()
    some = out.at[pl.ds(0, NXC - 1)]
    pltpu.make_async_copy(some, some, far_sem).wait()
    part = out.at[0, pl.ds(0, NZ - 1)]
    pltpu.make_async_copy(part, part, send_sem.at[0]).wait()
    pltpu.make_async_copy(some, some, send_sem.at[1]).wait()


def all_routes(meta):
    vmem = pl.BlockSpec(memory_space=pltpu.VMEM)
    return pl.pallas_call(
        routes_kernel,
        out_shape=jax.ShapeDtypeStruct((NXC, NZ) + meta.shape, meta.dtype),
        in_specs=[vmem],
        out_specs=vmem,
        scratch_shapes=[
            pltpu.SemaphoreType.DMA((2,)),
            pltpu.SemaphoreType.DMA,
            pltpu.SemaphoreType.DMA,
        ],
        compiler_params=pltpu.CompilerParams(collective_id=1, has_side_effects=True),
    )(meta)


def greet():
    z, xc, k = place()

    def along_z(d, carry):
        signal(lax.rem(z + d, NZ) * NXC + xc, k)
        return carry

    def in_plane(o, carry):
        signal(
            z * NXC + lax.rem(xc + lax.div(o, NB), NXC), lax.rem(k + lax.rem(o, NB), NB)
        )
        return carry

    lax.fori_loop(1, NZ, along_z, 0)
    lax.fori_loop(1, NXC * NB, in_plane, 0)
    pl.semaphore_wait(pltpu.get_barrier_semaphore(), NZ - 1 + NXC * NB - 1)


def whole_kernel(
    slots,
    lanes,
    table,
    panel,
    anc,
    parent_blocks,
    dinv,
    child_dinv,
    below_out,
    diag_out,
    column,
    child_diag,
    full,
    z_send,
    x_send,
    x,
    z_home,
    t_send,
    t_got,
    z_got,
    y_got,
    f_sem,
    fs_sem,
    fr_sem,
    zs_sem,
    zr_sem,
    xs_sem,
    xr_sem,
    ys_sem,
    yr_sem,
    hs_sem,
    hr_sem,
    ts_sem,
    tr_sem,
):
    z, xc, k = place()
    ancestors, width = parent_blocks.shape[0], parent_blocks.shape[-1]
    rows = width // NB
    count = column.shape[0]
    share = ancestors // NB
    cx, core = lax.div(xc, CORES), lax.rem(xc, CORES)
    plane = lax.rem(k - cx + NB, NB)

    def full_copy(i):
        return pltpu.make_async_copy(
            anc.at[i], full.at[0, i + 1, pl.ds(1, ancestors)], f_sem.at[i]
        )

    for i in range(ancestors):
        full_copy(i).start()
    greet()

    def ahead(n):
        return lax.rem(z + STEPS[n], NZ)

    def behind(n):
        return lax.rem(z + NZ - STEPS[n], NZ)

    def z_copy(n):
        return pltpu.make_async_remote_copy(
            src_ref=z_send.at[n],
            dst_ref=z_got[n],
            send_sem=zs_sem.at[n],
            recv_sem=zr_sem.at[n],
            device_id=(ahead(n) * NXC + xc, k),
            device_id_type=MESH,
        )

    def launch(n):
        def fill(j, carry):
            z_send[n, j] = panel[table[Z_CHILD + ahead(n) * PICKS + j]]
            return carry

        lax.fori_loop(0, slots, fill, 0)
        z_copy(n).start()

    for n in range(1, 1 + AT_ONCE):
        launch(n)

    def own(j, carry):
        z_got[0][j] = panel[table[Z_CHILD + z * PICKS + j]]
        return carry

    lax.fori_loop(0, slots, own, 0)

    def forward(n):
        if n:
            z_copy(n).wait_recv()

        def step(o, carry):
            other = lax.rem(cx + o, NX)
            row = lax.rem(other + n, NB)
            for lane in range(lanes):
                pick = table[X_PICK + behind(n) * PICKS + other * PAIR + lane]
                x_send[n * NX + other, lane] = z_got[n][pick]
            here = jnp.logical_and(o == 0, jnp.logical_and(core == n // NB, k == row))

            @pl.when(here)
            def _():
                pltpu.make_async_copy(
                    x_send.at[n * NX + other], x.at[xc, k], xr_sem.at[xc]
                ).start()

            @pl.when(jnp.logical_not(here))
            def _():
                pltpu.make_async_remote_copy(
                    src_ref=x_send.at[n * NX + other],
                    dst_ref=x.at[xc, k],
                    send_sem=xs_sem,
                    recv_sem=xr_sem.at[xc],
                    device_id=(z * NXC + other * CORES + n // NB, row),
                    device_id_type=MESH,
                ).start()

            return carry

        lax.fori_loop(0, NX, step, 0)

    sibling = pltpu.make_async_remote_copy(
        src_ref=full.at[0],
        dst_ref=full.at[1],
        send_sem=fs_sem,
        recv_sem=fr_sem,
        device_id=(z * NXC + cx * CORES + 1 - core, k),
        device_id_type=MESH,
    )

    def parent():
        diag = dinv[...].astype(F32)
        for i in range(ancestors):
            full_copy(i).wait()
            total = jnp.zeros((width, width), F32)
            for l in range(0, ancestors, NB):
                left = jnp.concatenate([full[0, i + 1, 1 + l + m] for m in range(NB)], axis=1)
                right = jnp.concatenate([parent_blocks[l + m] for m in range(NB)], axis=0)
                total += jnp.dot(left, right, preferred_element_type=F32)
            total = (-total).astype(BF16)
            full[0, i + 1, 0] = total
            full[0, 0, i + 1] = total.T
            diag -= lax.dot_general(
                parent_blocks[i], total, (((0,), (0,)), ((), ())), preferred_element_type=F32
            )
        full[0, 0, 0] = diag.astype(BF16)
        sibling.start()
        for i in range(share):
            below_out[i] = full[0, 1 + k * share + i, 0]
        diag_out[...] = full[0, 0, 0, pl.ds(k * rows, rows)]

    def children(half):
        landing = y_got[half].at[pl.ds((plane * NX + cx) * lanes, lanes)]
        sibling.wait_recv()

        def group(o, carry):
            other = lax.rem(xc + o, NXC)
            pltpu.make_async_copy(x.at[other], x.at[other], xr_sem.at[other]).wait()
            for lane in range(lanes):
                base = SPOTS + (other * PAIR + lane) * SPOT
                which = table[base]
                spot = [table[base + 1 + l] for l in range(NB)]
                right = jnp.concatenate([x[other, l, lane] for l in range(NB)], axis=0)
                for i in range(NB):
                    left = jnp.concatenate(
                        [full[which, spot[i], spot[l]] for l in range(NB)], axis=1
                    )
                    product = jnp.dot(left, right, preferred_element_type=F32)
                    x[other, i, lane] = (-product).astype(BF16)

            def back(i, carry):
                row = lax.rem(k + i, NB)
                here = jnp.logical_and(o == 0, i == 0)

                @pl.when(here)
                def _():
                    pltpu.make_async_copy(x.at[other, row], landing, yr_sem.at[half]).start()

                @pl.when(jnp.logical_not(here))
                def _():
                    pltpu.make_async_remote_copy(
                        src_ref=x.at[other, row],
                        dst_ref=landing,
                        send_sem=ys_sem,
                        recv_sem=yr_sem.at[half],
                        device_id=(z * NXC + other, row),
                        device_id_type=MESH,
                    ).start()

                return carry

            lax.fori_loop(0, NB, back, 0)
            return carry

        lax.fori_loop(0, NXC, group, 0)

    def home_copy(n, zone):
        return pltpu.make_async_remote_copy(
            src_ref=z_send.at[n],
            dst_ref=z_home.at[pl.ds(zone * slots, slots)],
            send_sem=hs_sem.at[n],
            recv_sem=hr_sem.at[n],
            device_id=(behind(n) * NXC + xc, k),
            device_id_type=MESH,
        )

    def backward(n):
        half, first = n // NB, n % NB * NX * lanes
        if n % NB == 0:
            pltpu.make_async_copy(y_got[half], y_got[half], yr_sem.at[half]).wait()
        if n:
            z_copy(n).wait_send()

        def pack(j, carry):
            block = y_got[half][first + table[Z_PICK + behind(n) * PICKS + j]]
            if n:
                z_send[n, j] = block
            else:
                z_home[z * slots + j] = block
            return carry

        lax.fori_loop(0, slots, pack, 0)
        if n:
            home_copy(n, z).start()

    forward(0)
    parent()
    for n in range(1, NB):
        forward(n)
        launch(n + AT_ONCE)
    launch(NZ - 1)

    @pl.when(core == 0)
    def _():
        children(0)

    for n in range(NB, NZ):
        forward(n)

    @pl.when(core == 1)
    def _():
        children(1)

    for n in range(NZ):
        backward(n)
    for n in range(1, NZ):
        home_copy(n, ahead(n)).wait_recv()

    batch = count // NB

    def term_copy(b, d):
        row = lax.rem(k + d, NB)
        return pltpu.make_async_remote_copy(
            src_ref=t_send.at[row, pl.ds(b * batch, batch)],
            dst_ref=t_got.at[k, pl.ds(b * batch, batch)],
            send_sem=ts_sem,
            recv_sem=tr_sem.at[b],
            device_id=(z * NXC + xc, row),
            device_id_type=MESH,
        )

    for b in range(NB):

        def unpack(i, carry):
            block = z_home[table[SLOT + i]]
            column[i] = block
            term = lax.dot_general(
                panel[i], block, (((0,), (0,)), ((), ())), preferred_element_type=F32
            )
            for q in range(NB):
                t_send[q, i] = term[q * rows : (q + 1) * rows]
            return carry

        lax.fori_loop(b * batch, (b + 1) * batch, unpack, 0)
        for d in range(1, NB):
            term_copy(b, d).start()

    for b in range(NB):
        got = t_got.at[pl.ds(0, NB - 1), pl.ds(b * batch, batch)]
        pltpu.make_async_copy(got, got, tr_sem.at[b]).wait()

        def finish(i, carry):
            total = t_send[k, i]
            for d in range(1, NB):
                total += t_got[lax.rem(k + d, NB), i]
            child_diag[i] = (child_dinv[i].astype(F32) - total).astype(BF16)
            return carry

        lax.fori_loop(b * batch, (b + 1) * batch, finish, 0)

    for n in range(1, NZ):
        home_copy(n, z).wait_send()
    remote = pl.ds(0, NZ * NX - 1)
    pltpu.make_async_copy(x_send.at[remote], x_send.at[remote], xs_sem).wait()
    pltpu.make_async_copy(x_send.at[remote], x_send.at[remote], ys_sem).wait()
    sibling.wait_send()
    sent = t_send.at[pl.ds(0, NB - 1)]
    pltpu.make_async_copy(sent, sent, ts_sem).wait()


def whole(slots, lanes, ident, table, panel_blocks, anc, parent_blocks, dinv, child_dinv):
    ancestors, width = parent_blocks.shape[0], parent_blocks.shape[-1]
    count, rows = panel_blocks.shape[0], width // NB
    block = (width, width)
    vmem = pl.BlockSpec(memory_space=pltpu.VMEM)
    dma = pltpu.SemaphoreType.DMA
    return pl.pallas_call(
        functools.partial(whole_kernel, slots, lanes),
        out_shape=(
            jax.ShapeDtypeStruct((ancestors // NB,) + block, BF16),
            jax.ShapeDtypeStruct((rows, width), BF16),
            jax.ShapeDtypeStruct((count,) + block, BF16),
            jax.ShapeDtypeStruct((count, rows, width), BF16),
        ),
        in_specs=[
            pl.BlockSpec(memory_space=pltpu.SMEM),
            vmem,
            pl.BlockSpec(memory_space=pl.ANY),
            vmem,
            vmem,
            vmem,
        ],
        out_specs=(vmem, vmem, vmem, vmem),
        scratch_shapes=[
            pltpu.VMEM((CORES, ancestors + 1, ancestors + 1) + block, BF16),
            pltpu.VMEM((NZ, slots) + block, BF16),
            pltpu.VMEM((NZ * NX, lanes) + block, BF16),
            pltpu.VMEM((NXC, NB, lanes) + block, BF16),
            pltpu.VMEM((NZ * slots,) + block, BF16),
            pltpu.VMEM((NB, count, rows, width), F32),
            pltpu.VMEM((NB, count, rows, width), F32),
            [pltpu.VMEM((slots,) + block, BF16) for _ in range(NZ)],
            [pltpu.VMEM((NB * NX * lanes,) + block, BF16) for _ in range(CORES)],
            dma((ancestors,)),
            dma,
            dma,
            dma((NZ,)),
            dma((NZ,)),
            dma,
            dma((NXC,)),
            dma,
            dma((CORES,)),
            dma((NZ,)),
            dma((NZ,)),
            dma,
            dma((NB,)),
        ],
        compiler_params=pltpu.CompilerParams(
            collective_id=ident, has_side_effects=True, vmem_limit_bytes=56 * 2**20
        ),
    )(table, panel_blocks, anc, parent_blocks, dinv, child_dinv)


def tables(child_route, child_pattern):
    z, xc, k = place()
    cx, core = lax.div(xc, CORES), lax.rem(xc, CORES)
    count = child_route.shape[0]
    meta = jnp.concatenate([child_route.reshape(-1), child_pattern.T.reshape(-1)])
    meta = jnp.pad(meta, (0, 8 * 128 - meta.shape[0])).reshape(8, 128)
    meta = all_routes(meta).reshape(NXC, NZ, -1)[..., : (1 + NB) * count]
    route = meta[..., :count]
    pattern = meta[..., count:].reshape(NXC, NZ, NB, count)
    goal = route // NXC
    earlier = jnp.arange(count)[None, :] < jnp.arange(count)[:, None]
    spot = jnp.sum(((goal[..., :, None] == goal[..., None, :]) & earlier).astype(jnp.int32), -1)
    chip = route // CORES
    rank = jnp.sum(((chip[..., :, None] == chip[..., None, :]) & earlier).astype(jnp.int32), -1)
    fullest, widest = jnp.max(spot) + 1, jnp.max(rank) + 1

    def of_xc(values):
        return lax.dynamic_index_in_dim(values, xc, 0, keepdims=False)

    places = jnp.arange(PICKS, dtype=jnp.int32)[:, None]
    route_xc, spot_xc, rank_xc = of_xc(route), of_xc(spot), of_xc(rank)
    goal_xc = route_xc // NXC
    own_goal = lax.dynamic_index_in_dim(goal_xc, z, 0, keepdims=False)
    own_spot = lax.dynamic_index_in_dim(spot_xc, z, 0, keepdims=False)
    hit = (own_goal == jnp.arange(NZ)[:, None, None]) & (own_spot == places)
    z_child = jnp.sum(jnp.where(hit, jnp.arange(count, dtype=jnp.int32), 0), -1)

    mine = (goal_xc == z)[:, None]
    lane_xc = rank_xc[:, None]
    chip_xc = (route_xc // CORES % NX)[:, None]
    via = spot_xc[:, None]
    x_pick = jnp.sum(jnp.where(mine & (chip_xc * PAIR + lane_xc == places), via, 0), -1)

    turn = core * NB + lax.rem(k - cx + NB, NB)
    step = jnp.sum(jnp.where(jnp.arange(NZ) == turn, jnp.array(STEPS, jnp.int32), 0))
    source = lax.rem(z - step + NZ, NZ)

    def of_source(values):
        return lax.dynamic_index_in_dim(values, source, 1, keepdims=False)

    there, lane = of_source(route), of_source(rank)
    hit = (there // CORES == z * NX + cx)[:, None] & (lane[:, None] == jnp.arange(PAIR)[:, None])
    which = (there % CORES != core).astype(jnp.int32)
    spots = jnp.concatenate([which[:, None], of_source(pattern)], axis=1)
    spots = jnp.sum(jnp.where(hit[:, :, None], spots[:, None], 0), -1)

    def with_slots(slots, lanes):
        z_pick = jnp.sum(jnp.where(mine & (via == places), chip_xc * lanes + lane_xc, 0), -1)
        parts = (z_child, x_pick, z_pick, spots, own_goal * slots + own_spot)
        return jnp.concatenate([part.reshape(-1) for part in parts])

    return fullest, widest, with_slots


def on_device(
    anc_inverse, parent_panel, parent_dinv, child_route, child_pattern, child_panel, child_dinv
):
    width = parent_dinv.shape[-1]
    ancestors = anc_inverse.shape[1]
    count = child_route.shape[0]
    fullest, widest, with_slots = tables(child_route, child_pattern)
    fits = [(fullest <= slots) & (widest <= lanes) for slots, lanes in SIZES[:-1]]
    size = jnp.int32(len(SIZES) - 1)
    for i in reversed(range(len(fits))):
        size = jnp.where(fits[i], i, size)
    slots = sum(jnp.where(size == i, SIZES[i][0], 0) for i in range(len(SIZES)))
    lanes = sum(jnp.where(size == i, SIZES[i][1], 0) for i in range(len(SIZES)))
    below, diag, column, child_diag = lax.switch(
        size,
        [functools.partial(whole, *SIZES[i], 2 + i) for i in range(len(SIZES))],
        with_slots(slots, lanes),
        child_panel.reshape(count, width, width),
        anc_inverse[0],
        parent_panel[0].reshape(ancestors, width, width),
        parent_dinv[0],
        child_dinv,
    )
    return (below.reshape(1, -1, width), diag[None], column, child_diag)


def solution(mesh):
    placed = (
        P("sn", None, None, None, None),
        P("sn", None, None),
        P("sn", None, None),
        P("sn", None),
        P("sn", None),
        P("sn", "br", None),
        P("sn", "br", None),
    )
    return jax.shard_map(
        on_device,
        mesh=mesh,
        in_specs=placed,
        out_specs=(
            P("sn", "br", None),
            P("sn", "br", None),
            P("sn", "br", None),
            P("sn", "br", None),
        ),
        check_vma=False,
    )
```

```python
import functools

import jax
import jax.numpy as jnp
from jax import lax
from jax.experimental import pallas as pl
from jax.experimental.pallas import tpu as pltpu
from jax.sharding import PartitionSpec as P

NZ = 8
NX = 4
CORES = 2
NXC = NX * CORES
NB = 4
CAP = 2
MESH = pl.DeviceIdType.MESH
BF16 = jnp.bfloat16
F32 = jnp.float32


STEPS = (0, 1, 7, 4, 3, 5, 2, 6)
AT_ONCE = 3
PICKS = NXC * CAP
PAIR = CORES * CAP
SIZES = ((6, 3), (7, 3), (8, 3), (PICKS, PAIR))
Z_CHILD = 0
X_PICK = Z_CHILD + NZ
Z_PICK = X_PICK + NZ
SPOTS = Z_PICK + NZ
SLOT = SPOTS + NXC
SIZE = SLOT + 8
SPOT = 1 + NB
LANES = 128


def place():
    sn = lax.axis_index("sn")
    return lax.div(sn, NXC), lax.rem(sn, NXC), lax.axis_index("br")


def signal(sn, row):
    pl.semaphore_signal(
        pltpu.get_barrier_semaphore(), inc=1, device_id=(sn, row), device_id_type=MESH
    )


def routes_kernel(route, pattern, table, meta, out, send_sem, near_sem, far_sem):
    z, xc, k = place()
    cx, core = lax.div(xc, CORES), lax.rem(xc, CORES)
    count = route.shape[0]

    def mate_z(d):
        return lax.rem(z + d, NZ) * NXC + xc

    def mate_xc(d):
        return z * NXC + lax.rem(xc + d, NXC)

    for d in range(1, NZ):
        signal(mate_z(d), k)
    for d in range(1, NXC):
        signal(mate_xc(d), k)

    fields = jnp.concatenate(
        [route[...], pattern[...], jnp.zeros((count, LANES - SPOT), jnp.int32)], axis=1
    )
    fields = jnp.concatenate([fields, jnp.zeros((LANES - count, LANES), jnp.int32)], axis=0)
    fields = fields.T[:8]
    lane = lax.broadcasted_iota(jnp.int32, (8, LANES), 1)
    low = lax.broadcasted_iota(jnp.int32, (8, LANES), 0)
    real = lane < count
    own = jnp.broadcast_to(fields[:1], (8, LANES))
    goal, chip = own // NXC, own // CORES
    spot, rank = jnp.zeros_like(own), jnp.zeros_like(own)
    for j in range(count):
        later = lane > j
        spot += (later & (goal == goal[:, j : j + 1])).astype(jnp.int32)
        rank += (later & (chip == chip[:, j : j + 1])).astype(jnp.int32)
    spot, rank = jnp.where(real, spot, 0), jnp.where(real, rank, 0)
    meta[...] = jnp.where(low == SPOT, spot, jnp.where(low == SPOT + 1, rank, fields))
    pl.semaphore_wait(pltpu.get_barrier_semaphore(), NZ + NXC - 2)

    pltpu.make_async_copy(meta, out.at[xc, z], near_sem).start()
    for d in range(1, NZ):
        pltpu.make_async_remote_copy(
            src_ref=meta,
            dst_ref=out.at[xc, z],
            send_sem=send_sem.at[0],
            recv_sem=near_sem,
            device_id=(mate_z(d), k),
            device_id_type=MESH,
        ).start()

    z_child = jnp.zeros((NZ, LANES), jnp.int32)
    for j in range(count):
        col = slice(j, j + 1)
        z_child += jnp.where((goal[:, col] == low) & (spot[:, col] == lane), j, 0)
    table[Z_CHILD : Z_CHILD + NZ] = z_child

    pltpu.make_async_copy(out.at[xc], out.at[xc], near_sem).wait()
    for d in range(1, NXC):
        pltpu.make_async_remote_copy(
            src_ref=out.at[xc],
            dst_ref=out.at[xc],
            send_sem=send_sem.at[1],
            recv_sem=far_sem,
            device_id=(mate_xc(d), k),
            device_id_type=MESH,
        ).start()
    some = out.at[pl.ds(0, NXC - 1)]
    pltpu.make_async_copy(some, some, far_sem).wait()
    part = out.at[0, pl.ds(0, NZ - 1)]
    pltpu.make_async_copy(part, part, send_sem.at[0]).wait()
    pltpu.make_async_copy(some, some, send_sem.at[1]).wait()

    most = out[0, 0]
    for q in range(1, NXC * NZ):
        most = jnp.maximum(most, out[q // NZ, q % NZ])
    fullest = jnp.max(most[SPOT : SPOT + 1], axis=1, keepdims=True) + 1
    widest = jnp.max(most[SPOT + 1 : SPOT + 2], axis=1, keepdims=True) + 1
    size = jnp.full((1, 1), len(SIZES) - 1, jnp.int32)
    slots = jnp.full((1, 1), SIZES[-1][0], jnp.int32)
    lanes = jnp.full((1, 1), SIZES[-1][1], jnp.int32)
    for i in reversed(range(len(SIZES) - 1)):
        fits = (fullest <= SIZES[i][0]) & (widest <= SIZES[i][1])
        size = jnp.where(fits, i, size)
        slots = jnp.where(fits, SIZES[i][0], slots)
        lanes = jnp.where(fits, SIZES[i][1], lanes)

    table[SLOT : SLOT + 8] = goal * slots + spot

    def rows(field):
        return jnp.concatenate([out[xc, q, field : field + 1] for q in range(NZ)], axis=0)

    there, spot, rank = rows(0), rows(SPOT), rows(SPOT + 1)
    goal, chip = there // NXC, there // CORES % NX
    x_key = jnp.where(goal == z, chip * PAIR + rank, -1)
    z_key = jnp.where(goal == z, spot, -1)
    z_value = chip * lanes + rank
    x_pick = jnp.zeros((NZ, LANES), jnp.int32)
    z_pick = jnp.zeros((NZ, LANES), jnp.int32)
    for j in range(count):
        col = slice(j, j + 1)
        x_pick += jnp.where(x_key[:, col] == lane, spot[:, col], 0)
        z_pick += jnp.where(z_key[:, col] == lane, z_value[:, col], 0)
    table[X_PICK : X_PICK + NZ] = x_pick
    table[Z_PICK : Z_PICK + NZ] = z_pick

    turn = core * NB + lax.rem(k - cx + NB, NB)
    step = jnp.int32(0)
    for i in range(NZ):
        step = jnp.where(turn == i, STEPS[i], step)
    source = lax.rem(z - step + NZ, NZ)
    there = [
        jnp.concatenate([out[q, source, f : f + 1] for q in range(NXC)], axis=0)
        for f in (*range(SPOT), SPOT + 1)
    ]
    chip, rank = there[0] // CORES, there[SPOT]
    key = jnp.where(chip == z * NX + cx, rank * SPOT, -SPOT)
    values = [(there[0] % CORES != core).astype(jnp.int32)] + there[1:SPOT]
    spots = jnp.zeros((NXC, LANES), jnp.int32)
    for j in range(count):
        col = slice(j, j + 1)
        for f in range(SPOT):
            spots += jnp.where(key[:, col] + f == lane, values[f][:, col], 0)
    table[SPOTS : SPOTS + NXC] = spots
    table[SIZE : SIZE + 8] = jnp.broadcast_to(size, (8, LANES))


def tables(route, pattern):
    vmem = pl.BlockSpec(memory_space=pltpu.VMEM)
    return pl.pallas_call(
        routes_kernel,
        out_shape=jax.ShapeDtypeStruct((SIZE + 8, LANES), jnp.int32),
        in_specs=[vmem, vmem],
        out_specs=vmem,
        scratch_shapes=[
            pltpu.VMEM((8, LANES), jnp.int32),
            pltpu.VMEM((NXC, NZ, 8, LANES), jnp.int32),
            pltpu.SemaphoreType.DMA((2,)),
            pltpu.SemaphoreType.DMA,
            pltpu.SemaphoreType.DMA,
        ],
        compiler_params=pltpu.CompilerParams(collective_id=1, has_side_effects=True),
    )(route, pattern)


def greet():
    z, xc, k = place()

    def along_z(d, carry):
        signal(lax.rem(z + d, NZ) * NXC + xc, k)
        return carry

    def in_plane(o, carry):
        signal(
            z * NXC + lax.rem(xc + lax.div(o, NB), NXC), lax.rem(k + lax.rem(o, NB), NB)
        )
        return carry

    lax.fori_loop(1, NZ, along_z, 0)
    lax.fori_loop(1, NXC * NB, in_plane, 0)
    pl.semaphore_wait(pltpu.get_barrier_semaphore(), NZ - 1 + NXC * NB - 1)


def whole_kernel(
    slots,
    lanes,
    table,
    panel,
    anc,
    parent_blocks,
    dinv,
    child_dinv,
    below_out,
    diag_out,
    column,
    child_diag,
    full,
    z_send,
    x_send,
    x,
    z_home,
    t_send,
    t_got,
    z_got,
    y_got,
    f_sem,
    fs_sem,
    fr_sem,
    zs_sem,
    zr_sem,
    xs_sem,
    xr_sem,
    ys_sem,
    yr_sem,
    hs_sem,
    hr_sem,
    ts_sem,
    tr_sem,
):
    z, xc, k = place()
    ancestors, width = parent_blocks.shape[0], parent_blocks.shape[-1]
    rows = width // NB
    count = column.shape[0]
    share = ancestors // NB
    cx, core = lax.div(xc, CORES), lax.rem(xc, CORES)
    plane = lax.rem(k - cx + NB, NB)

    def full_copy(i):
        return pltpu.make_async_copy(
            anc.at[i], full.at[0, i + 1, pl.ds(1, ancestors)], f_sem.at[i]
        )

    for i in range(ancestors):
        full_copy(i).start()
    greet()

    def ahead(n):
        return lax.rem(z + STEPS[n], NZ)

    def behind(n):
        return lax.rem(z + NZ - STEPS[n], NZ)

    def z_copy(n):
        return pltpu.make_async_remote_copy(
            src_ref=z_send.at[n],
            dst_ref=z_got[n],
            send_sem=zs_sem.at[n],
            recv_sem=zr_sem.at[n],
            device_id=(ahead(n) * NXC + xc, k),
            device_id_type=MESH,
        )

    def launch(n):
        def fill(j, carry):
            z_send[n, j] = panel[table[Z_CHILD + ahead(n), j]]
            return carry

        lax.fori_loop(0, slots, fill, 0)
        z_copy(n).start()

    for n in range(1, 1 + AT_ONCE):
        launch(n)

    def own(j, carry):
        z_got[0][j] = panel[table[Z_CHILD + z, j]]
        return carry

    lax.fori_loop(0, slots, own, 0)

    def forward(n):
        if n:
            z_copy(n).wait_recv()

        def step(o, carry):
            other = lax.rem(cx + o, NX)
            row = lax.rem(other + n, NB)
            for lane in range(lanes):
                pick = table[X_PICK + behind(n), other * PAIR + lane]
                x_send[n * NX + other, lane] = z_got[n][pick]
            here = jnp.logical_and(o == 0, jnp.logical_and(core == n // NB, k == row))

            @pl.when(here)
            def _():
                pltpu.make_async_copy(
                    x_send.at[n * NX + other], x.at[xc, k], xr_sem.at[xc]
                ).start()

            @pl.when(jnp.logical_not(here))
            def _():
                pltpu.make_async_remote_copy(
                    src_ref=x_send.at[n * NX + other],
                    dst_ref=x.at[xc, k],
                    send_sem=xs_sem,
                    recv_sem=xr_sem.at[xc],
                    device_id=(z * NXC + other * CORES + n // NB, row),
                    device_id_type=MESH,
                ).start()

            return carry

        lax.fori_loop(0, NX, step, 0)

    sibling = pltpu.make_async_remote_copy(
        src_ref=full.at[0],
        dst_ref=full.at[1],
        send_sem=fs_sem,
        recv_sem=fr_sem,
        device_id=(z * NXC + cx * CORES + 1 - core, k),
        device_id_type=MESH,
    )

    def parent():
        diag = dinv[...].astype(F32)
        for i in range(ancestors):
            full_copy(i).wait()
            total = jnp.zeros((width, width), F32)
            for l in range(0, ancestors, NB):
                left = jnp.concatenate([full[0, i + 1, 1 + l + m] for m in range(NB)], axis=1)
                right = jnp.concatenate([parent_blocks[l + m] for m in range(NB)], axis=0)
                total += jnp.dot(left, right, preferred_element_type=F32)
            total = (-total).astype(BF16)
            full[0, i + 1, 0] = total
            full[0, 0, i + 1] = total.T
            diag -= lax.dot_general(
                parent_blocks[i], total, (((0,), (0,)), ((), ())), preferred_element_type=F32
            )
        full[0, 0, 0] = diag.astype(BF16)
        sibling.start()
        for i in range(share):
            below_out[i] = full[0, 1 + k * share + i, 0]
        diag_out[...] = full[0, 0, 0, pl.ds(k * rows, rows)]

    def children(half):
        landing = y_got[half].at[pl.ds((plane * NX + cx) * lanes, lanes)]
        sibling.wait_recv()

        def group(o, carry):
            other = lax.rem(xc + o, NXC)
            pltpu.make_async_copy(x.at[other], x.at[other], xr_sem.at[other]).wait()
            for lane in range(lanes):
                which = table[SPOTS + other, lane * SPOT]
                spot = [table[SPOTS + other, lane * SPOT + 1 + l] for l in range(NB)]
                right = jnp.concatenate([x[other, l, lane] for l in range(NB)], axis=0)
                for i in range(NB):
                    left = jnp.concatenate(
                        [full[which, spot[i], spot[l]] for l in range(NB)], axis=1
                    )
                    product = jnp.dot(left, right, preferred_element_type=F32)
                    x[other, i, lane] = (-product).astype(BF16)

            def back(i, carry):
                row = lax.rem(k + i, NB)
                here = jnp.logical_and(o == 0, i == 0)

                @pl.when(here)
                def _():
                    pltpu.make_async_copy(x.at[other, row], landing, yr_sem.at[half]).start()

                @pl.when(jnp.logical_not(here))
                def _():
                    pltpu.make_async_remote_copy(
                        src_ref=x.at[other, row],
                        dst_ref=landing,
                        send_sem=ys_sem,
                        recv_sem=yr_sem.at[half],
                        device_id=(z * NXC + other, row),
                        device_id_type=MESH,
                    ).start()

                return carry

            lax.fori_loop(0, NB, back, 0)
            return carry

        lax.fori_loop(0, NXC, group, 0)

    def home_copy(n, zone):
        return pltpu.make_async_remote_copy(
            src_ref=z_send.at[n],
            dst_ref=z_home.at[pl.ds(zone * slots, slots)],
            send_sem=hs_sem.at[n],
            recv_sem=hr_sem.at[n],
            device_id=(behind(n) * NXC + xc, k),
            device_id_type=MESH,
        )

    def backward(n):
        half, first = n // NB, n % NB * NX * lanes
        if n in (3, 4):
            pltpu.make_async_copy(y_got[half], y_got[half], yr_sem.at[half]).wait()
        if n:
            z_copy(n).wait_send()

        def pack(j, carry):
            block = y_got[half][first + table[Z_PICK + behind(n), j]]
            if n:
                z_send[n, j] = block
            else:
                z_home[z * slots + j] = block
            return carry

        lax.fori_loop(0, slots, pack, 0)
        if n:
            home_copy(n, z).start()

    forward(0)
    parent()
    for n in range(1, NB):
        forward(n)
        launch(n + AT_ONCE)
    launch(NZ - 1)

    @pl.when(core == 0)
    def _():
        children(0)

    for n in range(NB, NZ):
        forward(n)

    @pl.when(core == 1)
    def _():
        children(1)

    for n in (3, 2, 1, 0, 4, 5, 6, 7):
        backward(n)
    for n in range(1, NZ):
        home_copy(n, ahead(n)).wait_recv()

    batch = count // NB

    def term_copy(b, d):
        row = lax.rem(k + d, NB)
        return pltpu.make_async_remote_copy(
            src_ref=t_send.at[row, pl.ds(b * batch, batch)],
            dst_ref=t_got.at[k, pl.ds(b * batch, batch)],
            send_sem=ts_sem,
            recv_sem=tr_sem.at[b],
            device_id=(z * NXC + xc, row),
            device_id_type=MESH,
        )

    for b in range(NB):

        def unpack(i, carry):
            block = z_home[table[SLOT, i]]
            column[i] = block
            term = lax.dot_general(
                panel[i], block, (((0,), (0,)), ((), ())), preferred_element_type=F32
            )
            for q in range(NB):
                t_send[q, i] = term[q * rows : (q + 1) * rows]
            return carry

        lax.fori_loop(b * batch, (b + 1) * batch, unpack, 0)
        for d in range(1, NB):
            term_copy(b, d).start()

    for b in range(NB):
        got = t_got.at[pl.ds(0, NB - 1), pl.ds(b * batch, batch)]
        pltpu.make_async_copy(got, got, tr_sem.at[b]).wait()

        def finish(i, carry):
            total = t_send[k, i]
            for d in range(1, NB):
                total += t_got[lax.rem(k + d, NB), i]
            child_diag[i] = (child_dinv[i].astype(F32) - total).astype(BF16)
            return carry

        lax.fori_loop(b * batch, (b + 1) * batch, finish, 0)

    for n in range(1, NZ):
        home_copy(n, z).wait_send()
    remote = pl.ds(0, NZ * NX - 1)
    pltpu.make_async_copy(x_send.at[remote], x_send.at[remote], xs_sem).wait()
    pltpu.make_async_copy(x_send.at[remote], x_send.at[remote], ys_sem).wait()
    sibling.wait_send()
    sent = t_send.at[pl.ds(0, NB - 1)]
    pltpu.make_async_copy(sent, sent, ts_sem).wait()


def whole(slots, lanes, ident, table, panel_blocks, anc, parent_blocks, dinv, child_dinv):
    ancestors, width = parent_blocks.shape[0], parent_blocks.shape[-1]
    count, rows = panel_blocks.shape[0], width // NB
    block = (width, width)
    vmem = pl.BlockSpec(memory_space=pltpu.VMEM)
    dma = pltpu.SemaphoreType.DMA
    return pl.pallas_call(
        functools.partial(whole_kernel, slots, lanes),
        out_shape=(
            jax.ShapeDtypeStruct((ancestors // NB,) + block, BF16),
            jax.ShapeDtypeStruct((rows, width), BF16),
            jax.ShapeDtypeStruct((count,) + block, BF16),
            jax.ShapeDtypeStruct((count, rows, width), BF16),
        ),
        in_specs=[
            pl.BlockSpec(memory_space=pltpu.SMEM),
            vmem,
            pl.BlockSpec(memory_space=pl.ANY),
            vmem,
            vmem,
            vmem,
        ],
        out_specs=(vmem, vmem, vmem, vmem),
        scratch_shapes=[
            pltpu.VMEM((CORES, ancestors + 1, ancestors + 1) + block, BF16),
            pltpu.VMEM((NZ, slots) + block, BF16),
            pltpu.VMEM((NZ * NX, lanes) + block, BF16),
            pltpu.VMEM((NXC, NB, lanes) + block, BF16),
            pltpu.VMEM((NZ * slots,) + block, BF16),
            pltpu.VMEM((NB, count, rows, width), F32),
            pltpu.VMEM((NB, count, rows, width), F32),
            [pltpu.VMEM((slots,) + block, BF16) for _ in range(NZ)],
            [pltpu.VMEM((NB * NX * lanes,) + block, BF16) for _ in range(CORES)],
            dma((ancestors,)),
            dma,
            dma,
            dma((NZ,)),
            dma((NZ,)),
            dma,
            dma((NXC,)),
            dma,
            dma((CORES,)),
            dma((NZ,)),
            dma((NZ,)),
            dma,
            dma((NB,)),
        ],
        compiler_params=pltpu.CompilerParams(
            collective_id=ident, has_side_effects=True, vmem_limit_bytes=56 * 2**20
        ),
    )(table, panel_blocks, anc, parent_blocks, dinv, child_dinv)


def on_device(
    anc_inverse, parent_panel, parent_dinv, child_route, child_pattern, child_panel, child_dinv
):
    width = parent_dinv.shape[-1]
    ancestors = anc_inverse.shape[1]
    count = child_route.shape[0]
    table = tables(child_route, child_pattern)
    below, diag, column, child_diag = lax.switch(
        table[SIZE, 0],
        [functools.partial(whole, *SIZES[i], 2 + i) for i in range(len(SIZES))],
        table,
        child_panel.reshape(count, width, width),
        anc_inverse[0],
        parent_panel[0].reshape(ancestors, width, width),
        parent_dinv[0],
        child_dinv,
    )
    return (below.reshape(1, -1, width), diag[None], column, child_diag)


def solution(mesh):
    placed = (
        P("sn", None, None, None, None),
        P("sn", None, None),
        P("sn", None, None),
        P("sn", None),
        P("sn", None),
        P("sn", "br", None),
        P("sn", "br", None),
    )
    return jax.shard_map(
        on_device,
        mesh=mesh,
        in_specs=placed,
        out_specs=(
            P("sn", "br", None),
            P("sn", "br", None),
            P("sn", "br", None),
            P("sn", "br", None),
        ),
        check_vma=False,
    )
```

```python
import functools

import jax
import jax.numpy as jnp
from jax import lax
from jax.experimental import pallas as pl
from jax.experimental.pallas import tpu as pltpu
from jax.sharding import PartitionSpec as P

NZ = 8
NX = 4
CORES = 2
NXC = NX * CORES
NB = 4
CAP = 2
MESH = pl.DeviceIdType.MESH
BF16 = jnp.bfloat16
F32 = jnp.float32


STEPS = (0, 1, 7, 4, 2, 6, 3, 5)
AT_ONCE = 3
PICKS = NXC * CAP
PAIR = CORES * CAP
SIZES = ((6, 3), (7, 3), (8, 3), (PICKS, PAIR))
Z_CHILD = 0
X_PICK = Z_CHILD + NZ
Z_PICK = X_PICK + NZ
SPOTS = Z_PICK + NZ
SLOT = SPOTS + NXC
SIZE = SLOT + 8
SPOT = 1 + NB
LANES = 128


def place():
    sn = lax.axis_index("sn")
    return lax.div(sn, NXC), lax.rem(sn, NXC), lax.axis_index("br")


def signal(sn, row):
    pl.semaphore_signal(
        pltpu.get_barrier_semaphore(), inc=1, device_id=(sn, row), device_id_type=MESH
    )


def routes_kernel(route, pattern, table, meta, out, send_sem, near_sem, far_sem):
    z, xc, k = place()
    cx, core = lax.div(xc, CORES), lax.rem(xc, CORES)
    count = route.shape[0]

    def mate_z(d):
        return lax.rem(z + d, NZ) * NXC + xc

    def mate_xc(d):
        return z * NXC + lax.rem(xc + d, NXC)

    for d in range(1, NZ):
        signal(mate_z(d), k)
    for d in range(1, NXC):
        signal(mate_xc(d), k)

    fields = jnp.concatenate(
        [route[...], pattern[...], jnp.zeros((count, LANES - SPOT), jnp.int32)], axis=1
    )
    fields = jnp.concatenate([fields, jnp.zeros((LANES - count, LANES), jnp.int32)], axis=0)
    fields = fields.T[:8]
    lane = lax.broadcasted_iota(jnp.int32, (8, LANES), 1)
    low = lax.broadcasted_iota(jnp.int32, (8, LANES), 0)
    real = lane < count
    own = jnp.broadcast_to(fields[:1], (8, LANES))
    goal, chip = own // NXC, own // CORES
    spot, rank = jnp.zeros_like(own), jnp.zeros_like(own)
    for j in range(count):
        later = lane > j
        spot += (later & (goal == goal[:, j : j + 1])).astype(jnp.int32)
        rank += (later & (chip == chip[:, j : j + 1])).astype(jnp.int32)
    spot, rank = jnp.where(real, spot, 0), jnp.where(real, rank, 0)
    meta[...] = jnp.where(low == SPOT, spot, jnp.where(low == SPOT + 1, rank, fields))
    pl.semaphore_wait(pltpu.get_barrier_semaphore(), NZ + NXC - 2)

    pltpu.make_async_copy(meta, out.at[xc, z], near_sem).start()
    for d in range(1, NZ):
        pltpu.make_async_remote_copy(
            src_ref=meta,
            dst_ref=out.at[xc, z],
            send_sem=send_sem.at[0],
            recv_sem=near_sem,
            device_id=(mate_z(d), k),
            device_id_type=MESH,
        ).start()

    z_child = jnp.zeros((NZ, LANES), jnp.int32)
    for j in range(count):
        col = slice(j, j + 1)
        z_child += jnp.where((goal[:, col] == low) & (spot[:, col] == lane), j, 0)
    table[Z_CHILD : Z_CHILD + NZ] = z_child

    pltpu.make_async_copy(out.at[xc], out.at[xc], near_sem).wait()
    for d in range(1, NXC):
        pltpu.make_async_remote_copy(
            src_ref=out.at[xc],
            dst_ref=out.at[xc],
            send_sem=send_sem.at[1],
            recv_sem=far_sem,
            device_id=(mate_xc(d), k),
            device_id_type=MESH,
        ).start()
    some = out.at[pl.ds(0, NXC - 1)]
    pltpu.make_async_copy(some, some, far_sem).wait()
    part = out.at[0, pl.ds(0, NZ - 1)]
    pltpu.make_async_copy(part, part, send_sem.at[0]).wait()
    pltpu.make_async_copy(some, some, send_sem.at[1]).wait()

    most = out[0, 0]
    for q in range(1, NXC * NZ):
        most = jnp.maximum(most, out[q // NZ, q % NZ])
    fullest = jnp.max(most[SPOT : SPOT + 1], axis=1, keepdims=True) + 1
    widest = jnp.max(most[SPOT + 1 : SPOT + 2], axis=1, keepdims=True) + 1
    size = jnp.full((1, 1), len(SIZES) - 1, jnp.int32)
    slots = jnp.full((1, 1), SIZES[-1][0], jnp.int32)
    lanes = jnp.full((1, 1), SIZES[-1][1], jnp.int32)
    for i in reversed(range(len(SIZES) - 1)):
        fits = (fullest <= SIZES[i][0]) & (widest <= SIZES[i][1])
        size = jnp.where(fits, i, size)
        slots = jnp.where(fits, SIZES[i][0], slots)
        lanes = jnp.where(fits, SIZES[i][1], lanes)

    table[SLOT : SLOT + 8] = goal * slots + spot

    def rows(field):
        return jnp.concatenate([out[xc, q, field : field + 1] for q in range(NZ)], axis=0)

    there, spot, rank = rows(0), rows(SPOT), rows(SPOT + 1)
    goal, chip = there // NXC, there // CORES % NX
    x_key = jnp.where(goal == z, chip * PAIR + rank, -1)
    z_key = jnp.where(goal == z, spot, -1)
    z_value = chip * lanes + rank
    x_pick = jnp.zeros((NZ, LANES), jnp.int32)
    z_pick = jnp.zeros((NZ, LANES), jnp.int32)
    for j in range(count):
        col = slice(j, j + 1)
        x_pick += jnp.where(x_key[:, col] == lane, spot[:, col], 0)
        z_pick += jnp.where(z_key[:, col] == lane, z_value[:, col], 0)
    table[X_PICK : X_PICK + NZ] = x_pick
    table[Z_PICK : Z_PICK + NZ] = z_pick

    turn = core * NB + lax.rem(k - cx + NB, NB)
    step = jnp.int32(0)
    for i in range(NZ):
        step = jnp.where(turn == i, STEPS[i], step)
    source = lax.rem(z - step + NZ, NZ)
    there = [
        jnp.concatenate([out[q, source, f : f + 1] for q in range(NXC)], axis=0)
        for f in (*range(SPOT), SPOT + 1)
    ]
    chip, rank = there[0] // CORES, there[SPOT]
    key = jnp.where(chip == z * NX + cx, rank * SPOT, -SPOT)
    values = [(there[0] % CORES != core).astype(jnp.int32)] + there[1:SPOT]
    spots = jnp.zeros((NXC, LANES), jnp.int32)
    for j in range(count):
        col = slice(j, j + 1)
        for f in range(SPOT):
            spots += jnp.where(key[:, col] + f == lane, values[f][:, col], 0)
    table[SPOTS : SPOTS + NXC] = spots
    table[SIZE : SIZE + 8] = jnp.broadcast_to(size, (8, LANES))


def tables(route, pattern):
    vmem = pl.BlockSpec(memory_space=pltpu.VMEM)
    return pl.pallas_call(
        routes_kernel,
        out_shape=jax.ShapeDtypeStruct((SIZE + 8, LANES), jnp.int32),
        in_specs=[vmem, vmem],
        out_specs=vmem,
        scratch_shapes=[
            pltpu.VMEM((8, LANES), jnp.int32),
            pltpu.VMEM((NXC, NZ, 8, LANES), jnp.int32),
            pltpu.SemaphoreType.DMA((2,)),
            pltpu.SemaphoreType.DMA,
            pltpu.SemaphoreType.DMA,
        ],
        compiler_params=pltpu.CompilerParams(collective_id=1, has_side_effects=True),
    )(route, pattern)


def greet():
    z, xc, k = place()

    def along_z(d, carry):
        signal(lax.rem(z + d, NZ) * NXC + xc, k)
        return carry

    def in_plane(o, carry):
        signal(
            z * NXC + lax.rem(xc + lax.div(o, NB), NXC), lax.rem(k + lax.rem(o, NB), NB)
        )
        return carry

    lax.fori_loop(1, NZ, along_z, 0)
    lax.fori_loop(1, NXC * NB, in_plane, 0)
    pl.semaphore_wait(pltpu.get_barrier_semaphore(), NZ - 1 + NXC * NB - 1)


def whole_kernel(
    slots,
    lanes,
    table,
    panel,
    anc,
    parent_blocks,
    dinv,
    child_dinv,
    below_out,
    diag_out,
    column,
    child_diag,
    full,
    z_send,
    x_send,
    x,
    z_home,
    t_send,
    t_got,
    z_got,
    y_got,
    f_sem,
    fs_sem,
    fr_sem,
    zs_sem,
    zr_sem,
    xs_sem,
    xr_sem,
    ys_sem,
    yr_sem,
    hs_sem,
    hr_sem,
    ts_sem,
    tr_sem,
):
    z, xc, k = place()
    ancestors, width = parent_blocks.shape[0], parent_blocks.shape[-1]
    rows = width // NB
    count = column.shape[0]
    share = ancestors // NB
    cx, core = lax.div(xc, CORES), lax.rem(xc, CORES)
    plane = lax.rem(k - cx + NB, NB)

    def full_copy(i):
        return pltpu.make_async_copy(
            anc.at[i], full.at[0, i + 1, pl.ds(1, ancestors)], f_sem.at[i]
        )

    for i in range(ancestors):
        full_copy(i).start()
    greet()

    def ahead(n):
        return lax.rem(z + STEPS[n], NZ)

    def behind(n):
        return lax.rem(z + NZ - STEPS[n], NZ)

    def z_copy(n):
        return pltpu.make_async_remote_copy(
            src_ref=z_send.at[n],
            dst_ref=z_got[n],
            send_sem=zs_sem.at[n],
            recv_sem=zr_sem.at[n],
            device_id=(ahead(n) * NXC + xc, k),
            device_id_type=MESH,
        )

    def launch(n):
        def fill(j, carry):
            z_send[n, j] = panel[table[Z_CHILD + ahead(n), j]]
            return carry

        lax.fori_loop(0, slots, fill, 0)
        z_copy(n).start()

    for n in range(1, 1 + AT_ONCE):
        launch(n)

    def own(j, carry):
        z_got[0][j] = panel[table[Z_CHILD + z, j]]
        return carry

    lax.fori_loop(0, slots, own, 0)

    def forward(n):
        if n:
            z_copy(n).wait_recv()

        def step(o, carry):
            other = lax.rem(cx + o, NX)
            row = lax.rem(other + n, NB)
            for lane in range(lanes):
                pick = table[X_PICK + behind(n), other * PAIR + lane]
                x_send[n * NX + other, lane] = z_got[n][pick]
            here = jnp.logical_and(o == 0, jnp.logical_and(core == n // NB, k == row))

            @pl.when(here)
            def _():
                pltpu.make_async_copy(
                    x_send.at[n * NX + other], x.at[xc, k], xr_sem.at[xc]
                ).start()

            @pl.when(jnp.logical_not(here))
            def _():
                pltpu.make_async_remote_copy(
                    src_ref=x_send.at[n * NX + other],
                    dst_ref=x.at[xc, k],
                    send_sem=xs_sem,
                    recv_sem=xr_sem.at[xc],
                    device_id=(z * NXC + other * CORES + n // NB, row),
                    device_id_type=MESH,
                ).start()

            return carry

        lax.fori_loop(0, NX, step, 0)

    sibling = pltpu.make_async_remote_copy(
        src_ref=full.at[0],
        dst_ref=full.at[1],
        send_sem=fs_sem,
        recv_sem=fr_sem,
        device_id=(z * NXC + cx * CORES + 1 - core, k),
        device_id_type=MESH,
    )

    def parent():
        diag = dinv[...].astype(F32)
        for i in range(ancestors):
            full_copy(i).wait()
            total = jnp.zeros((width, width), F32)
            for l in range(0, ancestors, NB):
                left = jnp.concatenate([full[0, i + 1, 1 + l + m] for m in range(NB)], axis=1)
                right = jnp.concatenate([parent_blocks[l + m] for m in range(NB)], axis=0)
                total += jnp.dot(left, right, preferred_element_type=F32)
            total = (-total).astype(BF16)
            full[0, i + 1, 0] = total
            full[0, 0, i + 1] = total.T
            diag -= lax.dot_general(
                parent_blocks[i], total, (((0,), (0,)), ((), ())), preferred_element_type=F32
            )
        full[0, 0, 0] = diag.astype(BF16)
        sibling.start()
        for i in range(share):
            below_out[i] = full[0, 1 + k * share + i, 0]
        diag_out[...] = full[0, 0, 0, pl.ds(k * rows, rows)]

    def children(half):
        landing = y_got[half].at[pl.ds((plane * NX + cx) * lanes, lanes)]
        sibling.wait_recv()

        def group(o, carry):
            other = lax.rem(xc + o, NXC)
            pltpu.make_async_copy(x.at[other], x.at[other], xr_sem.at[other]).wait()
            for lane in range(lanes):
                which = table[SPOTS + other, lane * SPOT]
                spot = [table[SPOTS + other, lane * SPOT + 1 + l] for l in range(NB)]
                right = jnp.concatenate([x[other, l, lane] for l in range(NB)], axis=0)
                for i in range(NB):
                    left = jnp.concatenate(
                        [full[which, spot[i], spot[l]] for l in range(NB)], axis=1
                    )
                    product = jnp.dot(left, right, preferred_element_type=F32)
                    x[other, i, lane] = (-product).astype(BF16)

            def back(i, carry):
                row = lax.rem(k + i, NB)
                here = jnp.logical_and(o == 0, i == 0)

                @pl.when(here)
                def _():
                    pltpu.make_async_copy(x.at[other, row], landing, yr_sem.at[half]).start()

                @pl.when(jnp.logical_not(here))
                def _():
                    pltpu.make_async_remote_copy(
                        src_ref=x.at[other, row],
                        dst_ref=landing,
                        send_sem=ys_sem,
                        recv_sem=yr_sem.at[half],
                        device_id=(z * NXC + other, row),
                        device_id_type=MESH,
                    ).start()

                return carry

            lax.fori_loop(0, NB, back, 0)
            return carry

        lax.fori_loop(0, NXC, group, 0)

    def home_copy(n, zone):
        return pltpu.make_async_remote_copy(
            src_ref=z_send.at[n],
            dst_ref=z_home.at[pl.ds(zone * slots, slots)],
            send_sem=hs_sem.at[n],
            recv_sem=hr_sem.at[n],
            device_id=(behind(n) * NXC + xc, k),
            device_id_type=MESH,
        )

    def backward(n):
        half, first = n // NB, n % NB * NX * lanes
        if n in (3, 6):
            pltpu.make_async_copy(y_got[half], y_got[half], yr_sem.at[half]).wait()
        if n:
            z_copy(n).wait_send()

        def pack(j, carry):
            block = y_got[half][first + table[Z_PICK + behind(n), j]]
            if n:
                z_send[n, j] = block
            else:
                z_home[z * slots + j] = block
            return carry

        lax.fori_loop(0, slots, pack, 0)
        if n:
            home_copy(n, z).start()

    forward(0)
    parent()
    for n in range(1, NB):
        forward(n)
        launch(n + AT_ONCE)
    launch(NZ - 1)

    @pl.when(core == 0)
    def _():
        children(0)

    for n in range(NB, NZ):
        forward(n)

    @pl.when(core == 1)
    def _():
        children(1)

    for n in (3, 2, 1, 0, 6, 7, 4, 5):
        backward(n)
    for n in range(1, NZ):
        home_copy(n, ahead(n)).wait_recv()

    batch = count // NB

    def term_copy(b, d):
        row = lax.rem(k + d, NB)
        return pltpu.make_async_remote_copy(
            src_ref=t_send.at[row, pl.ds(b * batch, batch)],
            dst_ref=t_got.at[k, pl.ds(b * batch, batch)],
            send_sem=ts_sem,
            recv_sem=tr_sem.at[b],
            device_id=(z * NXC + xc, row),
            device_id_type=MESH,
        )

    for b in range(NB):

        def unpack(i, carry):
            block = z_home[table[SLOT, i]]
            column[i] = block
            term = lax.dot_general(
                panel[i], block, (((0,), (0,)), ((), ())), preferred_element_type=F32
            )
            for q in range(NB):
                t_send[q, i] = term[q * rows : (q + 1) * rows]
            return carry

        lax.fori_loop(b * batch, (b + 1) * batch, unpack, 0)
        for d in range(1, NB):
            term_copy(b, d).start()

    for b in range(NB):
        got = t_got.at[pl.ds(0, NB - 1), pl.ds(b * batch, batch)]
        pltpu.make_async_copy(got, got, tr_sem.at[b]).wait()

        def finish(i, carry):
            total = t_send[k, i]
            for d in range(1, NB):
                total += t_got[lax.rem(k + d, NB), i]
            child_diag[i] = (child_dinv[i].astype(F32) - total).astype(BF16)
            return carry

        lax.fori_loop(b * batch, (b + 1) * batch, finish, 0)

    for n in range(1, NZ):
        home_copy(n, z).wait_send()
    remote = pl.ds(0, NZ * NX - 1)
    pltpu.make_async_copy(x_send.at[remote], x_send.at[remote], xs_sem).wait()
    pltpu.make_async_copy(x_send.at[remote], x_send.at[remote], ys_sem).wait()
    sibling.wait_send()
    sent = t_send.at[pl.ds(0, NB - 1)]
    pltpu.make_async_copy(sent, sent, ts_sem).wait()


def whole(slots, lanes, ident, table, panel_blocks, anc, parent_blocks, dinv, child_dinv):
    ancestors, width = parent_blocks.shape[0], parent_blocks.shape[-1]
    count, rows = panel_blocks.shape[0], width // NB
    block = (width, width)
    vmem = pl.BlockSpec(memory_space=pltpu.VMEM)
    dma = pltpu.SemaphoreType.DMA
    return pl.pallas_call(
        functools.partial(whole_kernel, slots, lanes),
        out_shape=(
            jax.ShapeDtypeStruct((ancestors // NB,) + block, BF16),
            jax.ShapeDtypeStruct((rows, width), BF16),
            jax.ShapeDtypeStruct((count,) + block, BF16),
            jax.ShapeDtypeStruct((count, rows, width), BF16),
        ),
        in_specs=[
            pl.BlockSpec(memory_space=pltpu.SMEM),
            vmem,
            pl.BlockSpec(memory_space=pl.ANY),
            vmem,
            vmem,
            vmem,
        ],
        out_specs=(vmem, vmem, vmem, vmem),
        scratch_shapes=[
            pltpu.VMEM((CORES, ancestors + 1, ancestors + 1) + block, BF16),
            pltpu.VMEM((NZ, slots) + block, BF16),
            pltpu.VMEM((NZ * NX, lanes) + block, BF16),
            pltpu.VMEM((NXC, NB, lanes) + block, BF16),
            pltpu.VMEM((NZ * slots,) + block, BF16),
            pltpu.VMEM((NB, count, rows, width), F32),
            pltpu.VMEM((NB, count, rows, width), F32),
            [pltpu.VMEM((slots,) + block, BF16) for _ in range(NZ)],
            [pltpu.VMEM((NB * NX * lanes,) + block, BF16) for _ in range(CORES)],
            dma((ancestors,)),
            dma,
            dma,
            dma((NZ,)),
            dma((NZ,)),
            dma,
            dma((NXC,)),
            dma,
            dma((CORES,)),
            dma((NZ,)),
            dma((NZ,)),
            dma,
            dma((NB,)),
        ],
        compiler_params=pltpu.CompilerParams(
            collective_id=ident, has_side_effects=True, vmem_limit_bytes=56 * 2**20
        ),
    )(table, panel_blocks, anc, parent_blocks, dinv, child_dinv)


def on_device(
    anc_inverse, parent_panel, parent_dinv, child_route, child_pattern, child_panel, child_dinv
):
    width = parent_dinv.shape[-1]
    ancestors = anc_inverse.shape[1]
    count = child_route.shape[0]
    table = tables(child_route, child_pattern)
    below, diag, column, child_diag = lax.switch(
        table[SIZE, 0],
        [functools.partial(whole, *SIZES[i], 2 + i) for i in range(len(SIZES))],
        table,
        child_panel.reshape(count, width, width),
        anc_inverse[0],
        parent_panel[0].reshape(ancestors, width, width),
        parent_dinv[0],
        child_dinv,
    )
    return (below.reshape(1, -1, width), diag[None], column, child_diag)


def solution(mesh):
    placed = (
        P("sn", None, None, None, None),
        P("sn", None, None),
        P("sn", None, None),
        P("sn", None),
        P("sn", None),
        P("sn", "br", None),
        P("sn", "br", None),
    )
    return jax.shard_map(
        on_device,
        mesh=mesh,
        in_specs=placed,
        out_specs=(
            P("sn", "br", None),
            P("sn", "br", None),
            P("sn", "br", None),
            P("sn", "br", None),
        ),
        check_vma=False,
    )
```

```python
import functools

import jax
import jax.numpy as jnp
from jax import lax
from jax.experimental import pallas as pl
from jax.experimental.pallas import tpu as pltpu
from jax.sharding import PartitionSpec as P

NZ = 8
NX = 4
CORES = 2
NXC = NX * CORES
NB = 4
CAP = 2
MESH = pl.DeviceIdType.MESH
BF16 = jnp.bfloat16
F32 = jnp.float32


STEPS = (0, 1, 7, 4, 3, 5, 2, 6)
AT_ONCE = 3
PICKS = NXC * CAP
PAIR = CORES * CAP
SIZES = ((6, 3), (7, 3), (8, 3), (PICKS, PAIR))
Z_CHILD = 0
X_PICK = Z_CHILD + NZ
Z_PICK = X_PICK + NZ
SPOTS = Z_PICK + NZ
SLOT = SPOTS + NXC
SIZE = SLOT + 8
SPOT = 1 + NB
LANES = 128


def place():
    sn = lax.axis_index("sn")
    return lax.div(sn, NXC), lax.rem(sn, NXC), lax.axis_index("br")


def signal(sn, row):
    pl.semaphore_signal(
        pltpu.get_barrier_semaphore(), inc=1, device_id=(sn, row), device_id_type=MESH
    )


def routes_kernel(route, pattern, table, meta, out, send_sem, near_sem, far_sem):
    z, xc, k = place()
    cx, core = lax.div(xc, CORES), lax.rem(xc, CORES)
    count = route.shape[1]

    def mate_z(d):
        return lax.rem(z + d, NZ) * NXC + xc

    def mate_xc(d):
        return z * NXC + lax.rem(xc + d, NXC)

    for d in range(1, NZ):
        signal(mate_z(d), k)
    for d in range(1, NXC):
        signal(mate_xc(d), k)

    meta[...] = jnp.zeros_like(meta)
    meta[0:1, :count] = route[...]
    meta[1:SPOT, :count] = pattern[...]
    fields = meta[...]
    lane = lax.broadcasted_iota(jnp.int32, (8, LANES), 1)
    low = lax.broadcasted_iota(jnp.int32, (8, LANES), 0)
    real = lane < count
    own = jnp.broadcast_to(fields[:1], (8, LANES))
    goal, chip = own // NXC, own // CORES
    spot, rank = jnp.zeros_like(own), jnp.zeros_like(own)
    for j in range(count):
        later = lane > j
        spot += (later & (goal == goal[:, j : j + 1])).astype(jnp.int32)
        rank += (later & (chip == chip[:, j : j + 1])).astype(jnp.int32)
    spot, rank = jnp.where(real, spot, 0), jnp.where(real, rank, 0)
    meta[...] = jnp.where(low == SPOT, spot, jnp.where(low == SPOT + 1, rank, fields))
    pl.semaphore_wait(pltpu.get_barrier_semaphore(), NZ + NXC - 2)

    pltpu.make_async_copy(meta, out.at[xc, z], near_sem).start()
    for d in range(1, NZ):
        pltpu.make_async_remote_copy(
            src_ref=meta,
            dst_ref=out.at[xc, z],
            send_sem=send_sem.at[0],
            recv_sem=near_sem,
            device_id=(mate_z(d), k),
            device_id_type=MESH,
        ).start()

    z_child = jnp.zeros((NZ, LANES), jnp.int32)
    for j in range(count):
        col = slice(j, j + 1)
        z_child += jnp.where((goal[:, col] == low) & (spot[:, col] == lane), j, 0)
    table[Z_CHILD : Z_CHILD + NZ] = z_child

    pltpu.make_async_copy(out.at[xc], out.at[xc], near_sem).wait()
    for d in range(1, NXC):
        pltpu.make_async_remote_copy(
            src_ref=out.at[xc],
            dst_ref=out.at[xc],
            send_sem=send_sem.at[1],
            recv_sem=far_sem,
            device_id=(mate_xc(d), k),
            device_id_type=MESH,
        ).start()
    some = out.at[pl.ds(0, NXC - 1)]
    pltpu.make_async_copy(some, some, far_sem).wait()
    part = out.at[0, pl.ds(0, NZ - 1)]
    pltpu.make_async_copy(part, part, send_sem.at[0]).wait()
    pltpu.make_async_copy(some, some, send_sem.at[1]).wait()

    most = out[0, 0]
    for q in range(1, NXC * NZ):
        most = jnp.maximum(most, out[q // NZ, q % NZ])
    fullest = jnp.max(most[SPOT : SPOT + 1], axis=1, keepdims=True) + 1
    widest = jnp.max(most[SPOT + 1 : SPOT + 2], axis=1, keepdims=True) + 1
    size = jnp.full((1, 1), len(SIZES) - 1, jnp.int32)
    slots = jnp.full((1, 1), SIZES[-1][0], jnp.int32)
    lanes = jnp.full((1, 1), SIZES[-1][1], jnp.int32)
    for i in reversed(range(len(SIZES) - 1)):
        fits = (fullest <= SIZES[i][0]) & (widest <= SIZES[i][1])
        size = jnp.where(fits, i, size)
        slots = jnp.where(fits, SIZES[i][0], slots)
        lanes = jnp.where(fits, SIZES[i][1], lanes)

    table[SLOT : SLOT + 8] = goal * slots + spot

    def rows(field):
        return jnp.concatenate([out[xc, q, field : field + 1] for q in range(NZ)], axis=0)

    there, spot, rank = rows(0), rows(SPOT), rows(SPOT + 1)
    goal, chip = there // NXC, there // CORES % NX
    x_key = jnp.where(goal == z, chip * PAIR + rank, -1)
    z_key = jnp.where(goal == z, spot, -1)
    z_value = chip * lanes + rank
    x_pick = jnp.zeros((NZ, LANES), jnp.int32)
    z_pick = jnp.zeros((NZ, LANES), jnp.int32)
    for j in range(count):
        col = slice(j, j + 1)
        x_pick += jnp.where(x_key[:, col] == lane, spot[:, col], 0)
        z_pick += jnp.where(z_key[:, col] == lane, z_value[:, col], 0)
    table[X_PICK : X_PICK + NZ] = x_pick
    table[Z_PICK : Z_PICK + NZ] = z_pick

    turn = core * NB + lax.rem(k - cx + NB, NB)
    step = jnp.int32(0)
    for i in range(NZ):
        step = jnp.where(turn == i, STEPS[i], step)
    source = lax.rem(z - step + NZ, NZ)
    there = [
        jnp.concatenate([out[q, source, f : f + 1] for q in range(NXC)], axis=0)
        for f in (*range(SPOT), SPOT + 1)
    ]
    chip, rank = there[0] // CORES, there[SPOT]
    key = jnp.where(chip == z * NX + cx, rank * SPOT, -SPOT)
    values = [(there[0] % CORES != core).astype(jnp.int32)] + there[1:SPOT]
    spots = jnp.zeros((NXC, LANES), jnp.int32)
    for j in range(count):
        col = slice(j, j + 1)
        for f in range(SPOT):
            spots += jnp.where(key[:, col] + f == lane, values[f][:, col], 0)
    table[SPOTS : SPOTS + NXC] = spots
    table[SIZE : SIZE + 8] = jnp.broadcast_to(size, (8, LANES))


def tables(route, pattern):
    vmem = pl.BlockSpec(memory_space=pltpu.VMEM)
    return pl.pallas_call(
        routes_kernel,
        out_shape=jax.ShapeDtypeStruct((SIZE + 8, LANES), jnp.int32),
        in_specs=[vmem, vmem],
        out_specs=vmem,
        scratch_shapes=[
            pltpu.VMEM((8, LANES), jnp.int32),
            pltpu.VMEM((NXC, NZ, 8, LANES), jnp.int32),
            pltpu.SemaphoreType.DMA((2,)),
            pltpu.SemaphoreType.DMA,
            pltpu.SemaphoreType.DMA,
        ],
        compiler_params=pltpu.CompilerParams(collective_id=1, has_side_effects=True),
    )(route, pattern)


def greet():
    z, xc, k = place()

    def along_z(d, carry):
        signal(lax.rem(z + d, NZ) * NXC + xc, k)
        return carry

    def in_plane(o, carry):
        signal(
            z * NXC + lax.rem(xc + lax.div(o, NB), NXC), lax.rem(k + lax.rem(o, NB), NB)
        )
        return carry

    lax.fori_loop(1, NZ, along_z, 0)
    lax.fori_loop(1, NXC * NB, in_plane, 0)
    pl.semaphore_wait(pltpu.get_barrier_semaphore(), NZ - 1 + NXC * NB - 1)


def whole_kernel(
    slots,
    lanes,
    table,
    panel,
    anc,
    parent_blocks,
    dinv,
    child_dinv,
    below_out,
    diag_out,
    column,
    child_diag,
    full,
    z_send,
    x_send,
    x,
    z_home,
    t_send,
    t_got,
    z_got,
    y_got,
    f_sem,
    fs_sem,
    fr_sem,
    zs_sem,
    zr_sem,
    xs_sem,
    xr_sem,
    ys_sem,
    yr_sem,
    hs_sem,
    hr_sem,
    ts_sem,
    tr_sem,
):
    z, xc, k = place()
    ancestors, width = parent_blocks.shape[0], parent_blocks.shape[-1]
    rows = width // NB
    count = column.shape[0]
    share = ancestors // NB
    cx, core = lax.div(xc, CORES), lax.rem(xc, CORES)
    plane = lax.rem(k - cx + NB, NB)

    def full_copy(i):
        return pltpu.make_async_copy(
            anc.at[i], full.at[0, i + 1, pl.ds(1, ancestors)], f_sem.at[i]
        )

    for i in range(ancestors):
        full_copy(i).start()
    greet()

    def ahead(n):
        return lax.rem(z + STEPS[n], NZ)

    def behind(n):
        return lax.rem(z + NZ - STEPS[n], NZ)

    def z_copy(n):
        return pltpu.make_async_remote_copy(
            src_ref=z_send.at[n],
            dst_ref=z_got[n],
            send_sem=zs_sem.at[n],
            recv_sem=zr_sem.at[n],
            device_id=(ahead(n) * NXC + xc, k),
            device_id_type=MESH,
        )

    def launch(n):
        def fill(j, carry):
            z_send[n, j] = panel[table[Z_CHILD + ahead(n), j]]
            return carry

        lax.fori_loop(0, slots, fill, 0)
        z_copy(n).start()

    for n in range(1, 1 + AT_ONCE):
        launch(n)

    def own(j, carry):
        z_got[0][j] = panel[table[Z_CHILD + z, j]]
        return carry

    lax.fori_loop(0, slots, own, 0)

    def forward(n):
        if n:
            z_copy(n).wait_recv()

        def step(o, carry):
            other = lax.rem(cx + o, NX)
            row = lax.rem(other + n, NB)
            for lane in range(lanes):
                pick = table[X_PICK + behind(n), other * PAIR + lane]
                x_send[n * NX + other, lane] = z_got[n][pick]
            here = jnp.logical_and(o == 0, jnp.logical_and(core == n // NB, k == row))

            @pl.when(here)
            def _():
                pltpu.make_async_copy(
                    x_send.at[n * NX + other], x.at[xc, k], xr_sem.at[xc]
                ).start()

            @pl.when(jnp.logical_not(here))
            def _():
                pltpu.make_async_remote_copy(
                    src_ref=x_send.at[n * NX + other],
                    dst_ref=x.at[xc, k],
                    send_sem=xs_sem,
                    recv_sem=xr_sem.at[xc],
                    device_id=(z * NXC + other * CORES + n // NB, row),
                    device_id_type=MESH,
                ).start()

            return carry

        lax.fori_loop(0, NX, step, 0)

    sibling = pltpu.make_async_remote_copy(
        src_ref=full.at[0],
        dst_ref=full.at[1],
        send_sem=fs_sem,
        recv_sem=fr_sem,
        device_id=(z * NXC + cx * CORES + 1 - core, k),
        device_id_type=MESH,
    )

    def parent():
        diag = dinv[...].astype(F32)
        for i in range(ancestors):
            full_copy(i).wait()
            total = jnp.zeros((width, width), F32)
            for l in range(0, ancestors, NB):
                left = jnp.concatenate([full[0, i + 1, 1 + l + m] for m in range(NB)], axis=1)
                right = jnp.concatenate([parent_blocks[l + m] for m in range(NB)], axis=0)
                total += jnp.dot(left, right, preferred_element_type=F32)
            total = (-total).astype(BF16)
            full[0, i + 1, 0] = total
            full[0, 0, i + 1] = total.T
            diag -= lax.dot_general(
                parent_blocks[i], total, (((0,), (0,)), ((), ())), preferred_element_type=F32
            )
        full[0, 0, 0] = diag.astype(BF16)
        sibling.start()
        for i in range(share):
            below_out[i] = full[0, 1 + k * share + i, 0]
        diag_out[...] = full[0, 0, 0, pl.ds(k * rows, rows)]

    def children(half):
        landing = y_got[half].at[pl.ds((plane * NX + cx) * lanes, lanes)]
        sibling.wait_recv()

        def group(o, carry):
            other = lax.rem(xc + o, NXC)
            pltpu.make_async_copy(x.at[other], x.at[other], xr_sem.at[other]).wait()
            for lane in range(lanes):
                which = table[SPOTS + other, lane * SPOT]
                spot = [table[SPOTS + other, lane * SPOT + 1 + l] for l in range(NB)]
                right = jnp.concatenate([x[other, l, lane] for l in range(NB)], axis=0)
                for i in range(NB):
                    left = jnp.concatenate(
                        [full[which, spot[i], spot[l]] for l in range(NB)], axis=1
                    )
                    product = jnp.dot(left, right, preferred_element_type=F32)
                    x[other, i, lane] = (-product).astype(BF16)

            def back(i, carry):
                row = lax.rem(k + i, NB)
                here = jnp.logical_and(o == 0, i == 0)

                @pl.when(here)
                def _():
                    pltpu.make_async_copy(x.at[other, row], landing, yr_sem.at[half]).start()

                @pl.when(jnp.logical_not(here))
                def _():
                    pltpu.make_async_remote_copy(
                        src_ref=x.at[other, row],
                        dst_ref=landing,
                        send_sem=ys_sem,
                        recv_sem=yr_sem.at[half],
                        device_id=(z * NXC + other, row),
                        device_id_type=MESH,
                    ).start()

                return carry

            lax.fori_loop(0, NB, back, 0)
            return carry

        lax.fori_loop(0, NXC, group, 0)

    def home_copy(n, zone):
        return pltpu.make_async_remote_copy(
            src_ref=z_send.at[n],
            dst_ref=z_home.at[pl.ds(zone * slots, slots)],
            send_sem=hs_sem.at[n],
            recv_sem=hr_sem.at[n],
            device_id=(behind(n) * NXC + xc, k),
            device_id_type=MESH,
        )

    def backward(n):
        half, first = n // NB, n % NB * NX * lanes
        if n in (3, 4):
            pltpu.make_async_copy(y_got[half], y_got[half], yr_sem.at[half]).wait()
        if n:
            z_copy(n).wait_send()

        def pack(j, carry):
            block = y_got[half][first + table[Z_PICK + behind(n), j]]
            if n:
                z_send[n, j] = block
            else:
                z_home[z * slots + j] = block
            return carry

        lax.fori_loop(0, slots, pack, 0)
        if n:
            home_copy(n, z).start()

    forward(0)
    parent()
    for n in range(1, NB):
        forward(n)
        launch(n + AT_ONCE)
    launch(NZ - 1)

    @pl.when(core == 0)
    def _():
        children(0)

    for n in range(NB, NZ):
        forward(n)

    @pl.when(core == 1)
    def _():
        children(1)

    for n in (3, 2, 1, 0, 4, 5, 6, 7):
        backward(n)
    for n in range(1, NZ):
        home_copy(n, ahead(n)).wait_recv()

    batch = count // NB

    def term_copy(b, d):
        row = lax.rem(k + d, NB)
        return pltpu.make_async_remote_copy(
            src_ref=t_send.at[row, pl.ds(b * batch, batch)],
            dst_ref=t_got.at[k, pl.ds(b * batch, batch)],
            send_sem=ts_sem,
            recv_sem=tr_sem.at[b],
            device_id=(z * NXC + xc, row),
            device_id_type=MESH,
        )

    for b in range(NB):

        def unpack(i, carry):
            block = z_home[table[SLOT, i]]
            column[i] = block
            term = lax.dot_general(
                panel[i], block, (((0,), (0,)), ((), ())), preferred_element_type=F32
            )
            for q in range(NB):
                t_send[q, i] = term[q * rows : (q + 1) * rows]
            return carry

        lax.fori_loop(b * batch, (b + 1) * batch, unpack, 0)
        for d in range(1, NB):
            term_copy(b, d).start()

    for b in range(NB):
        got = t_got.at[pl.ds(0, NB - 1), pl.ds(b * batch, batch)]
        pltpu.make_async_copy(got, got, tr_sem.at[b]).wait()

        def finish(i, carry):
            total = t_send[k, i]
            for d in range(1, NB):
                total += t_got[lax.rem(k + d, NB), i]
            child_diag[i] = (child_dinv[i].astype(F32) - total).astype(BF16)
            return carry

        lax.fori_loop(b * batch, (b + 1) * batch, finish, 0)

    for n in range(1, NZ):
        home_copy(n, z).wait_send()
    remote = pl.ds(0, NZ * NX - 1)
    pltpu.make_async_copy(x_send.at[remote], x_send.at[remote], xs_sem).wait()
    pltpu.make_async_copy(x_send.at[remote], x_send.at[remote], ys_sem).wait()
    sibling.wait_send()
    sent = t_send.at[pl.ds(0, NB - 1)]
    pltpu.make_async_copy(sent, sent, ts_sem).wait()


def whole(slots, lanes, ident, table, panel_blocks, anc, parent_blocks, dinv, child_dinv):
    ancestors, width = parent_blocks.shape[0], parent_blocks.shape[-1]
    count, rows = panel_blocks.shape[0], width // NB
    block = (width, width)
    vmem = pl.BlockSpec(memory_space=pltpu.VMEM)
    dma = pltpu.SemaphoreType.DMA
    return pl.pallas_call(
        functools.partial(whole_kernel, slots, lanes),
        out_shape=(
            jax.ShapeDtypeStruct((ancestors // NB,) + block, BF16),
            jax.ShapeDtypeStruct((rows, width), BF16),
            jax.ShapeDtypeStruct((count,) + block, BF16),
            jax.ShapeDtypeStruct((count, rows, width), BF16),
        ),
        in_specs=[
            pl.BlockSpec(memory_space=pltpu.SMEM),
            vmem,
            pl.BlockSpec(memory_space=pl.ANY),
            vmem,
            vmem,
            vmem,
        ],
        out_specs=(vmem, vmem, vmem, vmem),
        scratch_shapes=[
            pltpu.VMEM((CORES, ancestors + 1, ancestors + 1) + block, BF16),
            pltpu.VMEM((NZ, slots) + block, BF16),
            pltpu.VMEM((NZ * NX, lanes) + block, BF16),
            pltpu.VMEM((NXC, NB, lanes) + block, BF16),
            pltpu.VMEM((NZ * slots,) + block, BF16),
            pltpu.VMEM((NB, count, rows, width), F32),
            pltpu.VMEM((NB, count, rows, width), F32),
            [pltpu.VMEM((slots,) + block, BF16) for _ in range(NZ)],
            [pltpu.VMEM((NB * NX * lanes,) + block, BF16) for _ in range(CORES)],
            dma((ancestors,)),
            dma,
            dma,
            dma((NZ,)),
            dma((NZ,)),
            dma,
            dma((NXC,)),
            dma,
            dma((CORES,)),
            dma((NZ,)),
            dma((NZ,)),
            dma,
            dma((NB,)),
        ],
        compiler_params=pltpu.CompilerParams(
            collective_id=ident, has_side_effects=True, vmem_limit_bytes=56 * 2**20
        ),
    )(table, panel_blocks, anc, parent_blocks, dinv, child_dinv)


def on_device(
    anc_inverse, parent_panel, parent_dinv, child_route, child_pattern, child_panel, child_dinv
):
    width = parent_dinv.shape[-1]
    ancestors = anc_inverse.shape[1]
    count = child_route.shape[0]
    table = tables(child_route.T, child_pattern.T)
    below, diag, column, child_diag = lax.switch(
        table[SIZE, 0],
        [functools.partial(whole, *SIZES[i], 2 + i) for i in range(len(SIZES))],
        table,
        child_panel.reshape(count, width, width),
        anc_inverse[0],
        parent_panel[0].reshape(ancestors, width, width),
        parent_dinv[0],
        child_dinv,
    )
    return (below.reshape(1, -1, width), diag[None], column, child_diag)


def solution(mesh):
    placed = (
        P("sn", None, None, None, None),
        P("sn", None, None),
        P("sn", None, None),
        P("sn", None),
        P("sn", None),
        P("sn", "br", None),
        P("sn", "br", None),
    )
    return jax.shard_map(
        on_device,
        mesh=mesh,
        in_specs=placed,
        out_specs=(
            P("sn", "br", None),
            P("sn", "br", None),
            P("sn", "br", None),
            P("sn", "br", None),
        ),
        check_vma=False,
    )
```
